32 devices in a mesh: seq: 16 (over z, y, core), mp: 2 (over x).
Axes of the slice: x: 2, y: 2, z: 4, core: 2. Of those that a mesh axis runs over, the one named last changes fastest.
Arguments:
- x_in: bfloat16 [10240, 2048], P('seq'), may hold values from -6 to 6
- lengths: int32 [5], replicated, may hold values from 100 to 9640, as said below
- g_attn: float32 [2048], P('seq'), may hold values from 0.5 to 1.5
- w_query: float32 [2048, 2048], P('seq', 'mp'), may hold values from -0.125 to 0.125
- w_key: float32 [2048, 2048], P('seq', 'mp'), may hold values from -0.125 to 0.125
- w_value: float32 [2048, 2048], P('seq', 'mp'), may hold values from -0.125 to 0.125
- w_out: float32 [2048, 2048], P('mp', 'seq'), may hold values from -0.5 to 0.5
- g_ffn: float32 [2048], P('seq'), may hold values from 0.5 to 1.5
- w_gate: float32 [2048, 5504], P('seq', 'mp'), may hold values from -0.125 to 0.125
- w_up: float32 [2048, 5504], P('seq', 'mp'), may hold values from -0.125 to 0.125
- w_down: float32 [5504, 2048], P('mp', 'seq'), may hold values from -0.078125 to 0.078125
- cotangent: bfloat16 [10240, 2048], P('seq'), may hold values from -6 to 6
Outputs:
- out_act: bfloat16 [10240, 2048], P('seq')
- grad_input: bfloat16 [10240, 2048], P('seq')
- grad_g_attn: float32 [2048], P('seq')
- grad_w_query: float32 [2048, 2048], P('seq', 'mp')
- grad_w_key: float32 [2048, 2048], P('seq', 'mp')
- grad_w_value: float32 [2048, 2048], P('seq', 'mp')
- grad_w_out: float32 [2048, 2048], P('mp', 'seq')
- grad_g_ffn: float32 [2048], P('seq')
- grad_w_gate: float32 [2048, 5504], P('seq', 'mp')
- grad_w_up: float32 [2048, 5504], P('seq', 'mp')
- grad_w_down: float32 [5504, 2048], P('mp', 'seq')
The draws below stay inside these ranges and needn't reach their ends.
Inputs may be any that keep to these rules, and one draw needn't show every extreme that they name: 5 lengths in pack order summing to 10240; the entry at one place of 1 to 3, drawn from the seed, is the long sequence, of exactly 10240 - 4 // 2 * (300) tokens, which begins on the first index of seq and ends on the last; every other entry lies between 100 and 200, both taken in every draw, and these entries sum to 600.
All inputs are finite; a program needn't handle non-finite values.
Results may differ from the reference program's by a relative error of at most 0.015.
Values may be sent and summed in bfloat16 or wider, within the bound.
No kernel may reach another device: no remote copies, remote signals or barrier semaphores. Data moves between devices by JAX's collectives and lax.ppermute only.
A program may use at most 320 MiB of HBM per device.

```python
import math
import jax
import jax.numpy as jnp
from jax import lax

D = 2048
HEADS = 16
HEAD_DIM = 128
FF = 5504
WINDOW = 64
NSHORT = 4
SHORT_MAX = 200
TOKENS = 10240


def draw_lengths(key, part):
    key = jax.random.fold_in(key, 11)
    keys = jax.random.split(key, 3)
    least = SHORT_MAX // 2
    pair_total = SHORT_MAX + least
    halves = NSHORT // 2
    firsts = jax.random.randint(keys[0], (halves,), least, SHORT_MAX + 1)
    firsts = jnp.where(jnp.arange(halves, dtype=jnp.int32) == 0, SHORT_MAX, firsts)
    paired = jnp.concatenate([firsts, pair_total - firsts], 0).astype(jnp.int32)
    order = jax.random.permutation(keys[1], NSHORT)
    shorts = paired[order]
    place = jax.random.randint(keys[2], (), 1, NSHORT)
    longest = TOKENS - halves * pair_total
    index = jnp.arange(NSHORT + 1, dtype=jnp.int32)
    before = shorts[jnp.clip(index, 0, NSHORT - 1)]
    after = shorts[jnp.clip(index - 1, 0, NSHORT - 1)]
    return jnp.where(index < place, before, jnp.where(index == place, longest, after)).astype(jnp.int32)


def block_levels(own_key, shape, cuts, low, high):
    level = 1.0
    for dim, shards_of in cuts:
        steps = jax.random.uniform(jax.random.fold_in(jax.random.fold_in(own_key, 6), dim), (shards_of,), jnp.float32, low / len(cuts), high / len(cuts))
        level = level * jnp.repeat(jnp.exp(steps), shape[dim] // shards_of).reshape((-1,) + (1,) * (len(shape) - 1 - dim))
    return level


def gaussian(key, dims, scale, most, pieces=(), kind=jnp.bfloat16):
    values = scale * jax.random.normal(key, dims, jnp.float32)
    if pieces:
        values = values * block_levels(key, dims, pieces, -0.22, 0.18)
    return jnp.clip(values, -most, most).astype(kind)


def setup_inputs(seed: int = 0) -> dict:
    streams_of = jax.random.split(jax.random.key(seed), 13)
    x_in = gaussian(streams_of[0], (TOKENS, D), 1.0, 6.0, ((0, 16),))
    lengths = draw_lengths(jax.random.fold_in(streams_of[12], 71), 0)
    g_attn = jnp.clip(1.0 + 0.1 * jax.random.normal(streams_of[2], (D,), jnp.float32), 0.5, 1.5)
    w_query = gaussian(streams_of[3], (D, D), D ** -0.5, 0.125, ((0, 16), (1, 2)), jnp.float32)
    w_key = gaussian(streams_of[4], (D, D), D ** -0.5, 0.125, ((0, 16), (1, 2)), jnp.float32)
    w_value = gaussian(streams_of[5], (D, D), D ** -0.5, 0.125, ((0, 16), (1, 2)), jnp.float32)
    w_out = gaussian(streams_of[6], (D, D), (D // 16) ** -0.5, 0.5, ((0, 2), (1, 16)), jnp.float32)
    g_ffn = jnp.clip(1.0 + 0.1 * jax.random.normal(streams_of[7], (D,), jnp.float32), 0.5, 1.5)
    w_gate = gaussian(streams_of[8], (D, FF), D ** -0.5, 0.125, ((0, 16), (1, 2)), jnp.float32)
    w_up = gaussian(streams_of[9], (D, FF), D ** -0.5, 0.125, ((0, 16), (1, 2)), jnp.float32)
    w_down = gaussian(streams_of[10], (FF, D), FF ** -0.5, 0.078125, ((0, 2), (1, 16)), jnp.float32)
    cotangent = gaussian(streams_of[11], (TOKENS, D), 1.0, 6.0, ((0, 16),))
    return {"x_in": x_in, "lengths": lengths, "g_attn": g_attn, "w_query": w_query, "w_key": w_key, "w_value": w_value, "w_out": w_out, "g_ffn": g_ffn, "w_gate": w_gate, "w_up": w_up, "w_down": w_down, "cotangent": cotangent}


EPSILON = 1e-06
HIGHEST = lax.Precision.HIGHEST

@jax.custom_vjp
def low(v):
    return lax.optimization_barrier(v.astype(jnp.bfloat16)).astype(jnp.float32)

@jax.custom_vjp
def low_back(v):
    return v

def low_keep(v):
    return (low(v), None)

def low_pass(kept, grad):
    return (grad,)

def back_keep(v):
    return (v, None)

def back_low(kept, grad):
    return (low(grad),)
low.defvjp(low_keep, low_pass)
low_back.defvjp(back_keep, back_low)

def matmul(left, right):
    return jnp.dot(left, right, precision=HIGHEST, preferred_element_type=jnp.float32)

def rms_scale(values, gain):
    return values * lax.rsqrt(lax.optimization_barrier(jnp.mean(values * values, axis=-1, keepdims=True)) + EPSILON) * gain

def segment_of(lengths, count):
    bounds = jnp.cumsum(lengths)[:-1].astype(jnp.int32)
    places = jnp.arange(count, dtype=jnp.int32)
    return lax.optimization_barrier(jnp.sum((places[:, None] >= bounds[None, :]).astype(jnp.int32), axis=1)).astype(jnp.int32)

def attend_block(index, queries, key_pad, value_pad, seg_pad):
    block = 512
    score_scale = 1.0 / math.sqrt(HEAD_DIM)
    start = (index * block).astype(jnp.int32)
    query_blk = lax.dynamic_slice_in_dim(queries, start, block, 0).reshape(block, HEADS, HEAD_DIM)
    key_blk = lax.dynamic_slice_in_dim(key_pad, start, block + WINDOW, 0).reshape(block + WINDOW, HEADS, HEAD_DIM)
    value_blk = lax.dynamic_slice_in_dim(value_pad, start, block + WINDOW, 0).reshape(block + WINDOW, HEADS, HEAD_DIM)
    seg_query = lax.dynamic_slice_in_dim(seg_pad, (start + WINDOW).astype(jnp.int32), block, 0)
    seg_key = lax.dynamic_slice_in_dim(seg_pad, start, block + WINDOW, 0)
    row_ids = jnp.arange(block, dtype=jnp.int32)[:, None]
    col_ids = jnp.arange(block + WINDOW, dtype=jnp.int32)[None, :]
    allowed = (col_ids > row_ids) & (col_ids <= row_ids + WINDOW) & (seg_query[:, None] == seg_key[None, :])
    scores = low_back(jnp.einsum('qhd,khd->hqk', query_blk, key_blk, precision=HIGHEST) * score_scale)
    scores = jnp.where(allowed[None], scores, -1e+30)
    top = lax.optimization_barrier(jnp.max(scores, axis=-1, keepdims=True))
    weights = jnp.exp(scores - top)
    probs = low(weights / lax.optimization_barrier(jnp.sum(weights, axis=-1, keepdims=True)))
    return jnp.einsum('hqk,khd->qhd', probs, value_blk, precision=HIGHEST).reshape(block, D)

def banded_attention(queries, key_rows, value_rows, segments):
    total = queries.shape[0]
    count = total // 512
    pad_rows = jnp.zeros((WINDOW, D), jnp.float32)
    key_pad = jnp.concatenate([pad_rows, key_rows], 0)
    value_pad = jnp.concatenate([pad_rows, value_rows], 0)
    seg_pad = jnp.concatenate([jnp.full((WINDOW,), -1, jnp.int32), segments], 0)
    stepper = jax.checkpoint(attend_block)
    outputs = lax.map(lambda index: stepper(index, queries, key_pad, value_pad, seg_pad), jnp.arange(count, dtype=jnp.int32))
    return outputs.reshape(total, D)

def ffn_block(rows, gate_w, up_w, down_w):
    gate_pre = low_back(matmul(rows, gate_w))
    up_pre = low_back(matmul(rows, up_w))
    hidden = low(jax.nn.silu(gate_pre) * up_pre)
    return matmul(hidden, down_w)

def layer(x_full, g_attn, w_query, w_key, w_value, w_out, g_ffn, w_gate, w_up, w_down, segments):
    normed = low(rms_scale(x_full, low(g_attn)))
    queries = low(low_back(matmul(normed, low(w_query))))
    key_rows = low(low_back(matmul(normed, low(w_key))))
    value_rows = low(low_back(matmul(normed, low(w_value))))
    mixed = low(low_back(banded_attention(queries, key_rows, value_rows, segments)))
    branch = low_back(matmul(mixed, low(w_out)))
    middle = x_full + branch
    normed_two = low(rms_scale(middle, low(g_ffn)))
    gate_w = low(w_gate)
    up_w = low(w_up)
    down_w = low(w_down)
    block = math.gcd(x_full.shape[0], 4096)
    stepper = jax.checkpoint(ffn_block)
    ffn_out = lax.map(lambda rows: stepper(rows, gate_w, up_w, down_w), normed_two.reshape(-1, block, D)).reshape(-1, D)
    return middle + low_back(ffn_out)

def reference(x_in, lengths, g_attn, w_query, w_key, w_value, w_out, g_ffn, w_gate, w_up, w_down, cotangent):
    x_full = x_in.astype(jnp.float32)
    grad_out = cotangent.astype(jnp.float32)
    segments = segment_of(lengths, x_full.shape[0])

    def forward(x_full, g_attn, w_query, w_key, w_value, w_out, g_ffn, w_gate, w_up, w_down):
        return layer(x_full, g_attn, w_query, w_key, w_value, w_out, g_ffn, w_gate, w_up, w_down, segments)
    result, pullback = jax.vjp(forward, x_full, g_attn, w_query, w_key, w_value, w_out, g_ffn, w_gate, w_up, w_down)
    grads = pullback(grad_out)
    return (result.astype(jnp.bfloat16), grads[0].astype(jnp.bfloat16), grads[1], grads[2], grads[3], grads[4], grads[5], grads[6], grads[7], grads[8], grads[9])
```

```python
import functools
import math

import jax
import jax.numpy as jnp
from jax import lax
from jax.experimental import pallas as pl
from jax.experimental.pallas import tpu as pltpu
from jax.sharding import PartitionSpec as P

HEAD_DIM = 128
WINDOW = 64
EPSILON = 1e-06
BF16 = jnp.bfloat16
F32 = jnp.float32


def mat_nn(left, right):
    return jnp.dot(left, right, preferred_element_type=F32)


def mat_nt(left, right):
    return lax.dot_general(left, right, (((1,), (1,)), ((), ())), preferred_element_type=F32)


def mat_tn(left, right):
    return lax.dot_general(left, right, (((0,), (0,)), ((), ())), preferred_element_type=F32)


def shift_pairs(count, steps):
    return [(s, s + steps) for s in range(max(0, -steps), min(count, count - steps))]


def flip_pairs(count, bit):
    return [(s, s ^ bit) for s in range(count)]


def ring_pairs(count):
    return [(s, (s + 4) % count) for s in range(count)]


def relative_blocks(count):
    me = lax.axis_index("seq")
    place = jnp.arange(count, dtype=jnp.int32)
    outers = count // 4
    inner, middle, outer = place // (2 * outers), (place // outers) % 2, place % outers
    return (
        ((me // 4 + outer) % outers) * 4 + ((me // 2 + middle) % 2) * 2 + (me + inner) % 2
    ).astype(jnp.int32)


def rolled(values, steps, axis):
    return lax.dynamic_slice_in_dim(
        jnp.concatenate([values, values], axis), steps, values.shape[axis], axis
    )


def copy_block(order_ref, in_ref, out_ref):
    out_ref[...] = in_ref[...]


def to_relative(values, order):
    rows, columns = values.shape
    count = order.shape[0]
    width = columns // count
    if width % 128:
        me, outers = lax.axis_index("seq"), count // 4
        turned = rolled(values.reshape(rows, outers, 2, 2, width), me // 4, 1)
        turned = rolled(rolled(turned, (me // 2) % 2, 2), me % 2, 3)
        return jnp.transpose(turned, (0, 3, 2, 1, 4)).reshape(rows, columns)
    return pl.pallas_call(
        copy_block,
        grid_spec=pltpu.PrefetchScalarGridSpec(
            num_scalar_prefetch=1,
            grid=(count,),
            in_specs=[pl.BlockSpec((rows, width), lambda i, order: (0, order[i]))],
            out_specs=pl.BlockSpec((rows, width), lambda i, order: (0, i)),
        ),
        out_shape=jax.ShapeDtypeStruct(values.shape, values.dtype),
        cost_estimate=pl.CostEstimate(flops=0, bytes_accessed=4 * rows * columns, transcendentals=0),
    )(order, values)


def sum_to_owner(partial, kind=BF16):
    count = lax.axis_size("seq")
    outers = count // 4
    block = partial.shape[0] // count
    rest = partial.shape[1:]
    partial = partial.astype(kind).reshape((2, 2 * outers * block) + rest)
    got = lax.ppermute(partial[1], "seq", flip_pairs(count, 1))
    paired = (partial[0].astype(F32) + got.astype(F32)).astype(kind)
    paired = paired.reshape((2, outers * block) + rest)
    got = lax.ppermute(paired[1], "seq", flip_pairs(count, 2))
    four = (paired[0].astype(F32) + got.astype(F32)).astype(kind).reshape((outers, block) + rest)
    total = four[outers - 1]
    for r in range(outers - 2, -1, -1):
        got = lax.ppermute(total, "seq", ring_pairs(count))
        total = four[r].astype(F32) + got.astype(F32)
        if r:
            total = total.astype(kind)
    return total.astype(F32)


def sum_mp(partial):
    own = lax.optimization_barrier(partial.astype(BF16))
    count = lax.axis_size("mp")
    if count != 2:
        return lax.psum(own.astype(F32), "mp")
    other = lax.ppermute(own, "mp", [(0, 1), (1, 0)])
    return own.astype(F32) + other.astype(F32)


def attend(q_ref, k_ref, v_ref, bias_ref, out_ref):
    scale = 1.0 / math.sqrt(HEAD_DIM)
    for i in range(q_ref.shape[0] // WINDOW):
        rows, keys = slice(i * WINDOW, (i + 1) * WINDOW), slice(i * WINDOW, (i + 2) * WINDOW)
        scores = mat_nt(q_ref[rows], k_ref[keys]) * scale + bias_ref[rows]
        top = jnp.max(scores, axis=1, keepdims=True)
        weights = jnp.exp(scores - top)
        probs = weights / jnp.sum(weights, axis=1, keepdims=True)
        out_ref[rows] = mat_nn(probs.astype(BF16), v_ref[keys]).astype(BF16)


def attend_back(q_ref, k_ref, v_ref, bias_ref, da_ref, dq_ref, dk_ref, dv_ref):
    scale = 1.0 / math.sqrt(HEAD_DIM)
    steps = q_ref.shape[0] // WINDOW
    dk_low = dv_low = None
    for i in range(steps):
        rows, keys = slice(i * WINDOW, (i + 1) * WINDOW), slice(i * WINDOW, (i + 2) * WINDOW)
        query, key, value, da = q_ref[rows], k_ref[keys], v_ref[keys], da_ref[rows]
        scores = mat_nt(query, key) * scale + bias_ref[rows]
        top = jnp.max(scores, axis=1, keepdims=True)
        weights = jnp.exp(scores - top)
        probs = weights / jnp.sum(weights, axis=1, keepdims=True)
        dp = mat_nt(da, value)
        inner = jnp.sum(probs * dp, axis=1, keepdims=True)
        ds = (probs * (dp - inner)).astype(BF16)
        dv = mat_tn(probs.astype(BF16), da)
        dk = mat_tn(ds, query) * scale
        dq_ref[rows] = (mat_nn(ds, key) * scale).astype(BF16)
        if i:
            dk_ref[rows] = dk[:WINDOW] + dk_low
            dv_ref[rows] = dv[:WINDOW] + dv_low
        else:
            dk_ref[rows] = dk[:WINDOW]
            dv_ref[rows] = dv[:WINDOW]
        dk_low, dv_low = dk[WINDOW:], dv[WINDOW:]
    dk_ref[steps * WINDOW :] = dk_low
    dv_ref[steps * WINDOW :] = dv_low


def head_spec(rows):
    return pl.BlockSpec((rows, HEAD_DIM), lambda h: (0, h))


def attention_forward(queries, key_ext, value_ext, bias):
    tokens, width = queries.shape
    ext = tokens + WINDOW
    return pl.pallas_call(
        attend,
        grid=(width // HEAD_DIM,),
        in_specs=[
            head_spec(tokens),
            head_spec(ext),
            head_spec(ext),
            pl.BlockSpec((tokens, 2 * WINDOW), lambda h: (0, 0)),
        ],
        out_specs=head_spec(tokens),
        out_shape=jax.ShapeDtypeStruct((tokens, width), BF16),
        cost_estimate=pl.CostEstimate(
            flops=8 * tokens * width * WINDOW, bytes_accessed=8 * tokens * width, transcendentals=tokens * width
        ),
    )(queries, key_ext, value_ext, bias)


def attention_backward(queries, key_ext, value_ext, bias, da):
    tokens, width = queries.shape
    ext = tokens + WINDOW
    return pl.pallas_call(
        attend_back,
        grid=(width // HEAD_DIM,),
        in_specs=[
            head_spec(tokens),
            head_spec(ext),
            head_spec(ext),
            pl.BlockSpec((tokens, 2 * WINDOW), lambda h: (0, 0)),
            head_spec(tokens),
        ],
        out_specs=(head_spec(tokens), head_spec(ext), head_spec(ext)),
        out_shape=(
            jax.ShapeDtypeStruct((tokens, width), BF16),
            jax.ShapeDtypeStruct((ext, width), F32),
            jax.ShapeDtypeStruct((ext, width), F32),
        ),
        cost_estimate=pl.CostEstimate(
            flops=20 * tokens * width * WINDOW, bytes_accessed=20 * tokens * width, transcendentals=tokens * width
        ),
    )(queries, key_ext, value_ext, bias, da)


def norm_back(grad_normed, unit_rows, inverse_rows, gain):
    scaled = grad_normed * gain
    return inverse_rows * (scaled - unit_rows * jnp.mean(scaled * unit_rows, axis=1, keepdims=True))


def gather(shards):
    return lax.all_gather(jnp.concatenate([s.astype(BF16) for s in shards], 1), "seq", axis=0, tiled=True)


def per_device(
    x_in, lengths, g_attn, w_query, w_key, w_value, w_out, g_ffn, w_gate, w_up, w_down, cotangent
):
    tokens = x_in.shape[0]
    width = w_query.shape[1]
    ff = w_gate.shape[1]
    count = lax.axis_size("seq")
    cut = (ff // 2 + 127) // 128 * 128
    cuts = ((0, cut), (cut, ff))

    gains = lax.all_gather(jnp.stack([g_attn, g_ffn], 1).astype(BF16), "seq", axis=0, tiled=True)
    gain_one, gain_two = gains[:, 0].astype(F32), gains[:, 1].astype(F32)
    w_out_t, w_down_t = w_out.T, w_down.T
    attn_w = gather((w_query, w_key, w_value, w_out_t))
    ffn_w = [gather((w_gate[:, a:b], w_up[:, a:b], w_down_t[:, a:b])) for a, b in cuts]
    wqkv, wo_t = attn_w[:, : 3 * width], attn_w[:, 3 * width :]

    order = relative_blocks(count)
    first_place = lax.axis_index("seq") * tokens
    row = jnp.arange(tokens, dtype=jnp.int32)[:, None]
    column = jnp.arange(2 * WINDOW, dtype=jnp.int32)[None, :]
    key_place = row // WINDOW * WINDOW + column - WINDOW
    ends = [lengths[0]]
    for i in range(1, lengths.shape[0] - 1):
        ends.append(ends[-1] + lengths[i])
    seg_row = sum(((first_place + row) >= e).astype(jnp.int32) for e in ends)
    seg_key = sum(((first_place + key_place) >= e).astype(jnp.int32) for e in ends)
    allowed = (
        (key_place <= row)
        & (key_place > row - WINDOW)
        & (first_place + key_place >= 0)
        & (seg_row == seg_key)
    )
    bias = jnp.where(allowed, 0.0, -1e30).astype(F32)

    x_full = x_in.astype(F32)
    inverse_one = lax.rsqrt(jnp.mean(x_full * x_full, axis=1, keepdims=True) + EPSILON)
    unit_one = x_full * inverse_one
    normed = (unit_one * gain_one).astype(BF16)
    normed_rel = to_relative(normed, order)
    cot_rel = to_relative(cotangent, order)

    qkv = mat_nn(normed, wqkv).astype(BF16)
    queries = qkv[:, :width]
    tail = lax.ppermute(qkv[tokens - WINDOW :, width:], "seq", shift_pairs(count, 1))
    kv_ext = jnp.concatenate([tail, qkv[:, width:]], 0)
    key_ext, value_ext = kv_ext[:, :width], kv_ext[:, width:]
    mixed = attention_forward(queries, key_ext, value_ext, bias)
    middle = x_full + sum_mp(mat_nt(mixed, wo_t))
    inverse_two = lax.rsqrt(jnp.mean(middle * middle, axis=1, keepdims=True) + EPSILON)
    unit_two = middle * inverse_two
    normed_two = (unit_two * gain_two).astype(BF16)
    normed_two_rel = to_relative(normed_two, order)

    ffn_out = grad_normed_two = 0.0
    ffn_sums = []
    for (a, b), w in zip(cuts, ffn_w):
        n = b - a
        grad_hidden = mat_nn(cotangent, w[:, 2 * n :])
        gate_up = mat_nn(normed_two, w[:, : 2 * n])
        gate, up = gate_up[:, :n], gate_up[:, n:]
        sigma = jax.nn.sigmoid(gate)
        silu = gate * sigma
        hidden = (silu * up).astype(BF16)
        ffn_out = ffn_out + mat_nt(hidden, w[:, 2 * n :])
        grad_gate = (grad_hidden * up * sigma * (1.0 + gate * (1.0 - sigma))).astype(BF16)
        grad_up = (grad_hidden * silu).astype(BF16)
        grad_gate_up = jnp.concatenate([grad_gate, grad_up], 1)
        grad_normed_two = grad_normed_two + mat_nt(grad_gate_up, w[:, : 2 * n])
        grads = jnp.concatenate(
            [mat_tn(normed_two_rel, grad_gate_up).astype(BF16), mat_tn(cot_rel, hidden).astype(BF16)], 1
        )
        ffn_sums.append(sum_to_owner(grads))
    grad_normed_two = sum_mp(grad_normed_two)
    result = middle + sum_mp(ffn_out)
    grad_gain_two = jnp.sum(grad_normed_two * unit_two, axis=0)
    grad_middle = cotangent.astype(F32) + norm_back(grad_normed_two, unit_two, inverse_two, gain_two)
    grad_branch = grad_middle.astype(BF16)
    grad_branch_rel = to_relative(grad_branch, order)
    grad_wout_t = mat_tn(grad_branch_rel, mixed).astype(BF16)
    da = mat_nn(grad_branch, wo_t).astype(BF16)
    grad_query, dk_ext, dv_ext = attention_backward(queries, key_ext, value_ext, bias, da)
    back = lax.ppermute(
        jnp.concatenate([dk_ext[:WINDOW], dv_ext[:WINDOW]], 1).astype(BF16), "seq", shift_pairs(count, -1)
    ).astype(F32)

    def owned(ext, returned):
        return jnp.concatenate(
            [ext[WINDOW:tokens].astype(BF16), (ext[tokens:] + returned).astype(BF16)], 0
        )

    grad_key = owned(dk_ext, back[:, :width])
    grad_value = owned(dv_ext, back[:, width:])
    grad_qkv = jnp.concatenate([grad_query, grad_key, grad_value], 1)
    out_sum = sum_to_owner(grad_wout_t)
    qkv_sum = sum_to_owner(mat_tn(normed_rel, grad_qkv).astype(BF16))
    grad_normed = sum_mp(mat_nt(grad_qkv, wqkv))
    grad_gain_one = jnp.sum(grad_normed * unit_one, axis=0)
    grad_input = grad_middle + norm_back(grad_normed, unit_one, inverse_one, gain_one)
    gain_parts = jnp.stack([grad_gain_one, grad_gain_two], 0)
    gain_blocks = jnp.swapaxes(gain_parts.reshape(2, count, -1), 0, 1)
    chosen = order[:, None] == jnp.arange(count, dtype=jnp.int32)[None, :]
    gain_rel = jnp.sum(jnp.where(chosen[:, :, None, None], gain_blocks[None], 0.0), axis=1)
    gain_sums = sum_to_owner(gain_rel, F32)[0]

    def columns(part):
        pieces = []
        for (a, b), s in zip(cuts, ffn_sums):
            pieces.append(s[:, part * (b - a) : (part + 1) * (b - a)])
        return jnp.concatenate(pieces, 1)

    return (
        result.astype(BF16),
        grad_input.astype(BF16),
        gain_sums[0],
        qkv_sum[:, :width],
        qkv_sum[:, width : 2 * width],
        qkv_sum[:, 2 * width :],
        out_sum.T,
        gain_sums[1],
        columns(0),
        columns(1),
        columns(2).T,
    )


def solution(mesh):
    placed = (
        P("seq", None),
        P(),
        P("seq"),
        P("seq", "mp"),
        P("seq", "mp"),
        P("seq", "mp"),
        P("mp", "seq"),
        P("seq"),
        P("seq", "mp"),
        P("seq", "mp"),
        P("mp", "seq"),
        P("seq", None),
    )
    return jax.shard_map(
        per_device,
        mesh=mesh,
        in_specs=placed,
        out_specs=(
            P("seq", None),
            P("seq", None),
            P("seq"),
            P("seq", "mp"),
            P("seq", "mp"),
            P("seq", "mp"),
            P("mp", "seq"),
            P("seq"),
            P("seq", "mp"),
            P("seq", "mp"),
            P("mp", "seq"),
        ),
        check_vma=False,
    )
```

```python
import functools
import math

import jax
import jax.numpy as jnp
from jax import lax
from jax.experimental import pallas as pl
from jax.experimental.pallas import tpu as pltpu
from jax.sharding import PartitionSpec as P

HEAD_DIM = 128
WINDOW = 64
EPSILON = 1e-06
BF16 = jnp.bfloat16
F32 = jnp.float32
ANYWHERE = pl.BlockSpec(memory_space=pl.ANY)
HINT = 0.5


def cost(flops, bytes_accessed, transcendentals):
    return pl.CostEstimate(
        flops=int(HINT * flops),
        bytes_accessed=int(HINT * bytes_accessed),
        transcendentals=int(HINT * transcendentals),
    )


def mat_nn(left, right):
    return jnp.dot(left, right, preferred_element_type=F32)


def mat_nt(left, right):
    return lax.dot_general(left, right, (((1,), (1,)), ((), ())), preferred_element_type=F32)


def mat_tn(left, right):
    return lax.dot_general(left, right, (((0,), (0,)), ((), ())), preferred_element_type=F32)


def shift_pairs(count, steps):
    return [(s, s + steps) for s in range(max(0, -steps), min(count, count - steps))]


def flip_pairs(count, bit):
    return [(s, s ^ bit) for s in range(count)]


def relative_blocks(count):
    me = lax.axis_index("seq")
    place = jnp.arange(count, dtype=jnp.int32)
    outers = count // 4
    inner, middle, outer = place // (2 * outers), (place // outers) % 2, place % outers
    return (outer * 4 + ((me // 2 + middle) % 2) * 2 + (me + inner) % 2).astype(jnp.int32)


def rolled(values, steps, axis):
    return lax.dynamic_slice_in_dim(
        jnp.concatenate([values, values], axis), steps, values.shape[axis], axis
    )


def turn_blocks(pieces, order_ref, *refs):
    blocks = order_ref.shape[0] // 2
    first = 0
    for in_ref in refs[:pieces]:
        last = first + in_ref.shape[0]
        for half, out_ref in enumerate(refs[-2:]):
            for i in range(blocks):
                start = pl.multiple_of(order_ref[half * blocks + i] * 128, 128)
                out_ref[i * 128 : (i + 1) * 128, first:last] = in_ref[:, pl.ds(start, 128)].T
        first = last


def relative_turned(pieces, order, *after):
    rows, columns = sum(p.shape[0] for p in pieces), pieces[0].shape[1]
    count = order.shape[0]
    width = columns // count
    kind = pieces[0].dtype
    if width % 128:
        values = jnp.concatenate(pieces, 0)
        me, outers = lax.axis_index("seq"), count // 4
        turned = rolled(values.reshape(rows, outers, 2, 2, width), (me // 2) % 2, 2)
        turned = rolled(turned, me % 2, 3)
        return tuple(jnp.transpose(turned, (3, 2, 1, 4, 0)).reshape(2, columns // 2, rows))
    whole = pl.BlockSpec(memory_space=pltpu.VMEM)
    return pl.pallas_call(
        functools.partial(turn_blocks, len(pieces)),
        in_specs=[pl.BlockSpec(memory_space=pltpu.SMEM)] + [whole] * len(pieces) + [ANYWHERE] * len(after),
        out_specs=(whole, whole),
        out_shape=(jax.ShapeDtypeStruct((columns // 2, rows), kind),) * 2,
        cost_estimate=cost(flops=0, bytes_accessed=4 * rows * columns, transcendentals=0),
        compiler_params=pltpu.CompilerParams(vmem_limit_bytes=32 << 20),
    )(order, *pieces, *after)


def to_core(values):
    return lax.ppermute(values, "seq", flip_pairs(lax.axis_size("seq"), 1))


def to_middle(values):
    return lax.ppermute(values, "seq", flip_pairs(lax.axis_size("seq"), 2))


def sum_outer(values):
    outers = lax.axis_size("seq") // 4
    groups = [[o * 4 + place for o in range(outers)] for place in range(4)]
    return lax.psum_scatter(values, "seq", scatter_dimension=0, axis_index_groups=groups, tiled=True)


def add_block(keep_ref, got_ref, *refs):
    refs[-1][...] = (keep_ref[...].astype(F32) + got_ref[...].astype(F32)).astype(BF16)


def column_block(columns, most=1024):
    return next(w for w in range(most, 0, -128) if columns % w == 0)


def add_middle(part, after=()):
    keep, got = part[0], to_middle(part[1])
    rows, columns = keep.shape
    wide = column_block(columns)
    spec = pl.BlockSpec((rows, wide), lambda j: (0, j))
    return pl.pallas_call(
        add_block,
        grid=(columns // wide,),
        in_specs=[spec] * 2 + [ANYWHERE] * len(after),
        out_specs=spec,
        out_shape=jax.ShapeDtypeStruct((rows, columns), BF16),
        cost_estimate=cost(flops=rows * columns, bytes_accessed=6 * rows * columns, transcendentals=0),
        compiler_params=pltpu.CompilerParams(vmem_limit_bytes=32 << 20),
    )(keep, got, *after)


def sum_small(partial):
    count = lax.axis_size("seq")
    outers = count // 4
    rest = partial.shape[1:]
    partial = partial.reshape((2, 2 * outers) + rest)
    pair = partial[0] + to_core(partial[1])
    pair = pair.reshape((2, outers) + rest)
    four = pair[0] + to_middle(pair[1])
    outer = lax.axis_index("seq") // 4
    total = lax.dynamic_index_in_dim(four, outer, 0, keepdims=False)
    for step in range(1, outers):
        sent = lax.dynamic_index_in_dim(four, (outer + step) % outers, 0, keepdims=False)
        total = total + lax.ppermute(sent, "seq", [(s, (s + 4 * step) % count) for s in range(count)])
    return total


def bands(steps):
    return [
        (slice(i * WINDOW, (i + 1) * WINDOW), slice(i * WINDOW, (i + 2) * WINDOW)) for i in range(steps)
    ]


def band_probs(query, key, bias, steps):
    scale = 1.0 / math.sqrt(HEAD_DIM)
    scores = jnp.concatenate([mat_nt(query[rows], key[keys]) for rows, keys in bands(steps)], 0)
    scores = scores * scale + bias
    weights = jnp.exp(scores - jnp.max(scores, axis=1, keepdims=True))
    return weights / jnp.sum(weights, axis=1, keepdims=True)


def attend(q_ref, k_ref, v_ref, k_tail_ref, v_tail_ref, bias_ref, out_ref):
    steps = q_ref.shape[0] // WINDOW
    key = jnp.concatenate([k_tail_ref[...], k_ref[...]], 0)
    value = jnp.concatenate([v_tail_ref[...], v_ref[...]], 0)
    probs = band_probs(q_ref[...], key, bias_ref[...], steps).astype(BF16)
    for rows, keys in bands(steps):
        out_ref[rows] = mat_nn(probs[rows], value[keys]).astype(BF16)


def attend_back(heads, pieces, q_ref, k_ref, v_ref, k_tail_ref, v_tail_ref, bias_ref, *refs):
    dq_ref, dkv_ref, edge_send_ref, edge_keep_ref = refs[-4:]
    da = jnp.concatenate([r[...] for r in refs[:pieces]], 0)
    scale = 1.0 / math.sqrt(HEAD_DIM)
    head = pl.program_id(0)
    steps = q_ref.shape[0] // WINDOW
    query = q_ref[...]
    key = jnp.concatenate([k_tail_ref[...], k_ref[...]], 0)
    value = jnp.concatenate([v_tail_ref[...], v_ref[...]], 0)
    probs = band_probs(query, key, bias_ref[...], steps)
    dp = jnp.concatenate([mat_nt(da[rows], value[keys]) for rows, keys in bands(steps)], 0)
    inner = jnp.sum(probs * dp, axis=1, keepdims=True)
    ds = (probs * (dp - inner)).astype(BF16)
    probs = probs.astype(BF16)

    def place(part):
        return pl.ds(pl.multiple_of((part * heads + head) * HEAD_DIM, HEAD_DIM), HEAD_DIM)

    low = None
    for i, (rows, keys) in enumerate(bands(steps)):
        dq_ref[rows] = (mat_nn(ds[rows], key[keys]) * scale).astype(BF16)
        both = (mat_tn(ds[rows], query[rows]) * scale, mat_tn(probs[rows], da[rows]))
        for part in range(2):
            first = both[part][:WINDOW] if low is None else both[part][:WINDOW] + low[part]
            if i:
                dkv_ref[bands(steps)[i - 1][0], place(part)] = first.astype(BF16)
            else:
                edge_send_ref[:, place(part)] = first.astype(BF16)
        low = [b[WINDOW:] for b in both]
    for part in range(2):
        edge_keep_ref[:, place(part)] = low[part]


def head_spec(rows, first=0):
    return pl.BlockSpec((rows, HEAD_DIM), lambda h: (0, first + h))


def once(shape):
    return pl.BlockSpec(shape, lambda j: (0, 0), pipeline_mode=pl.Buffered(1))


def attention_specs(tokens, heads):
    return [
        head_spec(tokens),
        head_spec(tokens, heads),
        head_spec(tokens, 2 * heads),
        head_spec(WINDOW),
        head_spec(WINDOW, heads),
        once((tokens, 2 * WINDOW)),
    ]


def attention_forward(qkv, tail, bias):
    tokens, heads = qkv.shape[0], qkv.shape[1] // (3 * HEAD_DIM)
    width = heads * HEAD_DIM
    return pl.pallas_call(
        attend,
        grid=(heads,),
        in_specs=attention_specs(tokens, heads),
        out_specs=head_spec(tokens),
        out_shape=jax.ShapeDtypeStruct((tokens, width), BF16),
        cost_estimate=cost(
            flops=8 * tokens * width * WINDOW, bytes_accessed=8 * tokens * width, transcendentals=tokens * width
        ),
        compiler_params=pltpu.CompilerParams(vmem_limit_bytes=32 << 20),
    )(qkv, qkv, qkv, tail, tail, bias)


def attention_backward(qkv, tail, bias, da, *after):
    tokens, heads = qkv.shape[0], qkv.shape[1] // (3 * HEAD_DIM)
    width = heads * HEAD_DIM
    return pl.pallas_call(
        functools.partial(attend_back, heads, len(da)),
        grid=(heads,),
        in_specs=attention_specs(tokens, heads)
        + [head_spec(d.shape[0]) for d in da]
        + [ANYWHERE] * len(after),
        out_specs=(
            head_spec(tokens),
            once((tokens, 2 * width)),
            once((WINDOW, 2 * width)),
            once((WINDOW, 2 * width)),
        ),
        out_shape=(
            jax.ShapeDtypeStruct((tokens, width), BF16),
            jax.ShapeDtypeStruct((tokens, 2 * width), BF16),
            jax.ShapeDtypeStruct((WINDOW, 2 * width), BF16),
            jax.ShapeDtypeStruct((WINDOW, 2 * width), F32),
        ),
        cost_estimate=cost(
            flops=20 * tokens * width * WINDOW, bytes_accessed=14 * tokens * width, transcendentals=tokens * width
        ),
        compiler_params=pltpu.CompilerParams(vmem_limit_bytes=40 << 20),
    )(qkv, qkv, qkv, tail, tail, bias, *da, *after)


def multiply(turned, pieces, *refs):
    w_ref = refs[pieces]
    total, first = None, 0
    for x_ref in refs[:pieces]:
        last = first + x_ref.shape[1]
        term = mat_nt(x_ref[...], w_ref[:, first:last]) if turned else mat_nn(x_ref[...], w_ref[...])
        total = term if total is None else total + term
        first = last
    refs[-1][...] = total.astype(BF16)


def rows_times(pieces, weights, columns, first=0, turned=False, wide=512, after=()):
    tokens, d = pieces[0].shape[0], sum(p.shape[1] for p in pieces)
    if turned:
        out = weights.shape[0]
        spec = pl.BlockSpec((wide, columns), lambda j: (j, first // columns))
    else:
        out = columns
        spec = pl.BlockSpec((d, wide), lambda j: (0, first // wide + j))
    return pl.pallas_call(
        functools.partial(multiply, turned, len(pieces)),
        grid=(out // wide,),
        in_specs=[once(p.shape) for p in pieces] + [spec] + [ANYWHERE] * len(after),
        out_specs=pl.BlockSpec((tokens, wide), lambda j: (0, j)),
        out_shape=jax.ShapeDtypeStruct((tokens, out), BF16),
        cost_estimate=cost(
            flops=2 * tokens * d * out, bytes_accessed=2 * (tokens * (d + out) + d * out), transcendentals=0
        ),
        compiler_params=pltpu.CompilerParams(vmem_limit_bytes=48 << 20),
    )(*pieces, weights, *after)


PARTS = ((512, 3), (640, 2))


def feed(block, steps, first_row, h_ref, dm_ref, wgu_ref, wd_ref, *refs):
    j = pl.program_id(0)
    carried = first_row is not None
    if carried:
        m_in, dh_in = refs[:2]
        wide_ref, hidden_ref, m_out, dh_out, m_sum, dh_sum = refs[-6:]
    else:
        wide_ref, hidden_ref, m_sum, dh_sum = refs[-4:]
    gate_up = mat_nn(h_ref[...], wgu_ref[...])
    gate, up = gate_up[:, :block], gate_up[:, block:]
    dhidden = mat_nn(dm_ref[...], wd_ref[...])
    sigma = jax.nn.sigmoid(gate)
    silu = gate * sigma
    hidden = (silu * up).astype(BF16)
    dup = (dhidden * silu).astype(BF16)
    dgate = (dhidden * up * (sigma * (1.0 + gate * (1.0 - sigma)))).astype(BF16)
    dgate_up = jnp.concatenate([dgate, dup], 1)
    wide_ref[...] = dgate_up
    hidden_ref[...] = hidden

    @pl.when(j == 0)
    def _():
        if carried:
            rows = pl.ds(first_row, m_sum.shape[0])
            pltpu.sync_copy(m_in.at[rows], m_sum)
            pltpu.sync_copy(dh_in.at[rows], dh_sum)
        else:
            m_sum[...] = jnp.zeros_like(m_sum)
            dh_sum[...] = jnp.zeros_like(dh_sum)

    width = 512
    for c in range(0, m_sum.shape[1], width):
        part = slice(c, c + width)
        dh_sum[:, part] += mat_nt(dgate_up, wgu_ref[part])
        m_sum[:, part] += mat_nt(hidden, wd_ref[part])

    if carried:

        @pl.when(j == steps - 1)
        def _():
            m_out[...] = m_sum[...].astype(BF16)
            dh_out[...] = dh_sum[...].astype(BF16)


def feed_forward(rows, dm, weights, part, carry=(), place=0, count=1, after=()):
    d = rows.shape[1]
    block, steps = part
    wide = steps * block
    carried = bool(carry)
    tokens = count * 128 if carried else rows.shape[0]
    row_spec = once((tokens, d))
    if carried:
        rows, dm = rows[place * 128 : place * 128 + tokens], dm[place * 128 : place * 128 + tokens]
    kind = BF16 if carried else F32
    return pl.pallas_call(
        functools.partial(feed, block, steps, place * 128 if carried else None),
        grid=(steps,),
        in_specs=[
            row_spec,
            row_spec,
            pl.BlockSpec((d, 2 * block), lambda j: (0, j)),
            pl.BlockSpec((d, block), lambda j: (0, 2 * steps + j)),
        ]
        + [ANYWHERE] * (len(carry) + len(after)),
        out_specs=(
            pl.BlockSpec((tokens, 2 * block), lambda j: (0, j)),
            pl.BlockSpec((tokens, block), lambda j: (0, j)),
            row_spec,
            row_spec,
        ),
        out_shape=(
            jax.ShapeDtypeStruct((tokens, 2 * wide), BF16),
            jax.ShapeDtypeStruct((tokens, wide), BF16),
            jax.ShapeDtypeStruct((tokens, d), kind),
            jax.ShapeDtypeStruct((tokens, d), kind),
        ),
        scratch_shapes=[pltpu.VMEM((tokens, d), F32)] * 2 if carried else [],
        cost_estimate=cost(
            flops=12 * tokens * d * wide, bytes_accessed=6 * d * wide + 24 * tokens * d, transcendentals=tokens * wide
        ),
        compiler_params=pltpu.CompilerParams(vmem_limit_bytes=60 << 20),
    )(rows, dm, weights, weights, *carry, *after)


def grad_block(pieces, outers, left_ref, left_got_ref, *refs):
    keep_ref, send_ref = refs[-2:]
    total = None
    for side, left in enumerate((left_ref, left_got_ref)):
        first = 0
        for right in refs[side * pieces : (side + 1) * pieces]:
            last = first + right.shape[0]
            term = mat_nn(left[:, first:last], right[...])
            total = term if total is None else total + term
            first = last
    total = total.astype(BF16)
    half = total.shape[0] // 2
    if not outers:
        keep_ref[...] = total[:half]
        send_ref[...] = total[half:]
        return
    block = half // outers
    for i in range(2 * outers):
        first = (i % 2) * half + (i // 2) * block
        send_ref[i * block : (i + 1) * block] = total[first : first + block]


def weight_grad(left, right, after=(), first=0, columns=None, outers=0):
    d, tokens = left[0].shape
    columns = columns or right[0][0].shape[1]
    wide = next(w for w in (640, 512, 256, 128) if columns % w == 0 and first % w == 0)
    pieces = tuple(right[0]) + tuple(right[1])
    outs = (jax.ShapeDtypeStruct((d, columns), BF16),)
    if not outers:
        outs = (jax.ShapeDtypeStruct((d // 2, columns), BF16),) * 2
    return pl.pallas_call(
        functools.partial(grad_block, len(right[0]), outers),
        grid=(columns // wide,),
        in_specs=[once((d, tokens))] * 2
        + [pl.BlockSpec((p.shape[0], wide), lambda j: (0, first // wide + j)) for p in pieces]
        + [ANYWHERE] * len(after),
        out_specs=(pl.BlockSpec((d // len(outs), wide), lambda j: (0, j)),) * len(outs),
        out_shape=outs,
        cost_estimate=cost(
            flops=4 * tokens * d * columns, bytes_accessed=2 * (d + 2 * tokens) * columns + 4 * d * tokens, transcendentals=0
        ),
        compiler_params=pltpu.CompilerParams(vmem_limit_bytes=48 << 20),
    )(*left, *pieces, *after)


def middle_back(own_ref, got_ref, middle_ref, dm_ref, gain_ref, wo_ref, *refs):
    grad_ref, low_ref, da_ref, gain_out = refs[-4:]
    rows = middle_ref[...]
    inverse = lax.rsqrt(jnp.mean(rows * rows, axis=1, keepdims=True) + EPSILON)
    unit = rows * inverse
    dh = own_ref[...].astype(F32) + got_ref[...].astype(F32)
    grad = dm_ref[...].astype(F32) + norm_back(dh, unit, inverse, gain_ref[...])
    grad_ref[...] = grad
    low = grad.astype(BF16)
    low_ref[...] = low
    da_ref[...] = mat_nn(low, wo_ref[...]).astype(BF16)
    part = jnp.sum(dh * unit, axis=0, keepdims=True)

    @pl.when(pl.program_id(0) == 0)
    def _():
        gain_out[...] = part

    @pl.when(pl.program_id(0) > 0)
    def _():
        gain_out[...] += part


def middle_gradient(own, got, middle, dm, gain, weights, width, place, after=()):
    tokens, d = own.shape

    def rows(first, n=d):
        return pl.BlockSpec((128, n), lambda i: (first + i, 0))

    return pl.pallas_call(
        middle_back,
        grid=(tokens // 128,),
        in_specs=[
            rows(0),
            rows(0),
            rows(place),
            rows(place),
            once((1, d)),
            pl.BlockSpec((d, width), lambda i: (0, 3), pipeline_mode=pl.Buffered(1)),
        ]
        + [ANYWHERE] * len(after),
        out_specs=(rows(0), rows(0), rows(0, width), once((1, d))),
        out_shape=(
            jax.ShapeDtypeStruct((tokens, d), F32),
            jax.ShapeDtypeStruct((tokens, d), BF16),
            jax.ShapeDtypeStruct((tokens, width), BF16),
            jax.ShapeDtypeStruct((1, d), F32),
        ),
        cost_estimate=cost(
            flops=2 * tokens * d * width, bytes_accessed=2 * d * width + 16 * tokens * d, transcendentals=0
        ),
        compiler_params=pltpu.CompilerParams(vmem_limit_bytes=48 << 20),
    )(own, got, middle, dm, gain, weights, *after)


def norm_back(grad_normed, unit_rows, inverse_rows, gain):
    scaled = grad_normed * gain
    return inverse_rows * (scaled - unit_rows * jnp.mean(scaled * unit_rows, axis=1, keepdims=True))


def gather(shards):
    return lax.all_gather(jnp.concatenate(shards, 1), "seq", axis=0, tiled=True)


def per_device(
    x_in, lengths, g_attn, w_query, w_key, w_value, w_out, g_ffn, w_gate, w_up, w_down, cotangent
):
    tokens = x_in.shape[0]
    width = w_query.shape[1]
    ff = w_gate.shape[1]
    count = lax.axis_size("seq")
    def rounded(shard, a=0, b=None):
        shard = shard.astype(BF16)
        b = shard.shape[1] if b is None else b
        pad = max(0, b - shard.shape[1])
        return jnp.pad(shard[:, a:b], ((0, 0), (0, pad)))

    def zeros(n):
        return jnp.zeros((w_query.shape[0], n), BF16)

    w_down_t = w_down.astype(BF16).T
    gains_here = rounded(jnp.stack([g_attn, g_ffn], 1), 0, 128)
    attn_w = gather(
        (rounded(w_query), rounded(w_key), rounded(w_value), w_out.astype(BF16).T, gains_here)
    )
    ffn_w = []
    a = 0
    for block, steps in PARTS:
        wide = [rounded(w, a + j * block, a + (j + 1) * block) for j in range(steps) for w in (w_gate, w_up)]
        wide.append(rounded(w_down_t, a, a + steps * block))
        spare = 4224 - 3 * steps * block
        ffn_w.append(gather(wide + ([zeros(spare)] if spare > 0 else [])))
        a += steps * block
    gains = attn_w[:, 4 * width : 4 * width + 2].T.astype(F32)
    gain_one, gain_two = gains[0], gains[1]

    order = relative_blocks(count)
    first_place = lax.axis_index("seq") * tokens
    row = jnp.arange(tokens, dtype=jnp.int32)[:, None]
    column = jnp.arange(2 * WINDOW, dtype=jnp.int32)[None, :]
    key_place = row // WINDOW * WINDOW + column - WINDOW
    ends = [lengths[0]]
    for i in range(1, lengths.shape[0] - 1):
        ends.append(ends[-1] + lengths[i])
    seg_row = sum(((first_place + row) >= e).astype(jnp.int32) for e in ends)
    seg_key = sum(((first_place + key_place) >= e).astype(jnp.int32) for e in ends)
    allowed = (
        (key_place <= row)
        & (key_place > row - WINDOW)
        & (first_place + key_place >= 0)
        & (seg_row == seg_key)
    )
    bias = jnp.where(allowed, 0.0, -1e30).astype(F32)

    x_full = x_in.astype(F32)
    inverse_one = lax.rsqrt(jnp.mean(x_full * x_full, axis=1, keepdims=True) + EPSILON)
    unit_one = x_full * inverse_one
    def both_halves(pieces, *after):
        own, other = relative_turned(pieces, order, *after)
        return own, to_core(other)

    def both_cores(*pieces):
        return pieces, tuple(to_core(p) for p in pieces)

    def to_mp(own):
        return lax.ppermute(own, "mp", [(0, 1), (1, 0)])

    cot_turned = both_halves((cotangent,))
    normed = (unit_one * gain_one).astype(BF16)
    normed_turned = both_halves((normed,))

    qkv = rows_times((normed,), attn_w, 3 * width)
    tail = lax.ppermute(qkv[tokens - WINDOW :, width:], "seq", shift_pairs(count, 1))
    mixed = attention_forward(qkv, tail, bias)
    mixed_both = both_cores(mixed)
    branch = rows_times((mixed,), attn_w, width, 3 * width, True)
    middle = x_full + (branch.astype(F32) + to_mp(branch).astype(F32))
    inverse_two = lax.rsqrt(jnp.mean(middle * middle, axis=1, keepdims=True) + EPSILON)
    normed_two = (middle * inverse_two * gain_two).astype(BF16)
    normed_two_turned = both_halves((normed_two,))

    after = (mixed_both[1][0], cot_turned[1], normed_turned[1])
    one, two = (block * steps for block, steps in PARTS)
    wide_acts, hidden, *carry = feed_forward(normed_two, cotangent, ffn_w[0], PARTS[0], after=after)
    wide_acts = both_cores(wide_acts)
    one_a = weight_grad(normed_two_turned, wide_acts, (), 0, one)
    one_c = weight_grad(cot_turned, both_cores(hidden), one_a, outers=count // 4)
    one_b = weight_grad(normed_two_turned, wide_acts, one_c, one, one)
    one_c = sum_outer(one_c[0])
    places = ((0, (tokens // 128 + 1) // 2), ((tokens // 128 + 1) // 2, tokens // 256))
    after = one_b
    halves = []
    for place, blocks in places:
        halves.append(feed_forward(normed_two, cotangent, ffn_w[1], PARTS[1], tuple(carry), place, blocks, after))
        if not place:
            one_a = add_middle(one_a, (halves[0][0],))
            after = (one_a,)
    wide_acts, hidden, m_halves, dh_halves = zip(*halves)
    after = (wide_acts[1],)
    wide_acts, hidden = both_cores(*wide_acts), both_cores(*hidden)
    middles = []
    for (place, _), dh in zip(places, dh_halves):
        middles.append(
            middle_gradient(dh, to_mp(dh), middle, cotangent, gain_two[None], attn_w, width, place, after)
        )
        if not place:
            one_b = add_middle(one_b, (middles[0][1], one_c))
            two_a = weight_grad(normed_two_turned, wide_acts, (one_b,), 0, two)
            after = two_a
    grad_gain_two = sum(m[3][0] for m in middles)
    two_b = weight_grad(normed_two_turned, wide_acts, (middles[1][1],), two, two)
    two_a = add_middle(two_a, two_b)
    half = one_c.shape[0] // 2
    one_c = one_c[:half].astype(F32) + to_middle(one_c[half:]).astype(F32)
    one_a, one_b = sum_outer(one_a), sum_outer(one_b)
    branch_turned = both_halves([m[1] for m in middles], two_a)
    grad_q, grad_kv, edge_send, edge_keep = attention_backward(
        qkv, tail, bias, [m[2] for m in middles], branch_turned[0]
    )
    two_c = weight_grad(cot_turned, hidden, (edge_keep,))
    two_b = add_middle(two_b, two_c)
    after = (two_b, one_a)
    two_a, two_b = sum_outer(two_a), sum_outer(two_b)
    two_c = add_middle(two_c, after)
    q_part = weight_grad(normed_turned, both_cores(grad_q), (two_c, one_b))
    out_part = weight_grad(branch_turned, mixed_both, q_part)
    two_c = sum_outer(two_c)
    late, _ = lax.optimization_barrier((m_halves, branch_turned[0]))
    late = jnp.concatenate(late, 0)
    late_got = to_mp(late)
    edge_keep, _ = lax.optimization_barrier((edge_keep, out_part[0]))
    back = lax.ppermute(edge_send, "seq", shift_pairs(count, -1))
    last_rows = (edge_keep + back.astype(F32)).astype(BF16)
    grad_kv = lax.dynamic_update_slice(grad_kv, last_rows, (tokens - WINDOW, 0))
    kv_both = both_cores(grad_kv)
    k_part = weight_grad(normed_turned, kv_both, (late_got, *out_part), 0, width)
    v_part = weight_grad(normed_turned, kv_both, k_part, width, width)
    q_part = add_middle(q_part, (*v_part, two_a))
    own = rows_times((grad_q, grad_kv), attn_w, 3 * width, 0, True, after=(q_part,))
    own_got = to_mp(own)
    out_part = add_middle(out_part, (own, two_b))
    k_part = add_middle(k_part, (out_part, two_c))
    v_part = add_middle(v_part, (k_part, own_got))
    q_sum, out_sum = sum_outer(q_part).astype(F32), sum_outer(out_part).astype(F32)
    k_sum, v_sum = sum_outer(k_part).astype(F32), sum_outer(v_part).astype(F32)
    grad_normed = own.astype(F32) + own_got.astype(F32)
    grad_gain_one = jnp.sum(own.astype(F32) * unit_one, axis=0)
    grad_gain_one = grad_gain_one + to_mp(grad_gain_one)
    grad_middle = jnp.concatenate([m[0] for m in middles], 0)
    grad_input = grad_middle + norm_back(grad_normed, unit_one, inverse_one, gain_one)
    result = middle + (late.astype(F32) + late_got.astype(F32))
    gain_parts = jnp.stack([grad_gain_one, grad_gain_two], 0)
    gain_blocks = jnp.swapaxes(gain_parts.reshape(2, count, -1), 0, 1)
    chosen = order[:, None] == jnp.arange(count, dtype=jnp.int32)[None, :]
    gain_rel = jnp.sum(jnp.where(chosen[:, :, None, None], gain_blocks[None], 0.0), axis=1)
    gain_sums = sum_small(gain_rel)

    wide_one, wide_two = jnp.concatenate([one_a, one_b], 1), jnp.concatenate([two_a, two_b], 1)

    def columns(which):
        pieces = []
        for (block, steps), wide in zip(PARTS, (wide_one, wide_two)):
            pieces += [wide[:, (2 * j + which) * block : (2 * j + which + 1) * block] for j in range(steps)]
        return jnp.concatenate(pieces, 1)[:, :ff].astype(F32)

    grad_gate, grad_up = columns(0), columns(1)
    grad_down = jnp.concatenate([one_c, two_c.astype(F32)], 1)[:, :ff].astype(F32)

    return (
        result.astype(BF16),
        grad_input.astype(BF16),
        gain_sums[0],
        q_sum,
        k_sum,
        v_sum,
        out_sum.T,
        gain_sums[1],
        grad_gate,
        grad_up,
        grad_down.T,
    )


def solution(mesh):
    placed = (
        P("seq", None),
        P(),
        P("seq"),
        P("seq", "mp"),
        P("seq", "mp"),
        P("seq", "mp"),
        P("mp", "seq"),
        P("seq"),
        P("seq", "mp"),
        P("seq", "mp"),
        P("mp", "seq"),
        P("seq", None),
    )
    return jax.shard_map(
        per_device,
        mesh=mesh,
        in_specs=placed,
        out_specs=(
            P("seq", None),
            P("seq", None),
            P("seq"),
            P("seq", "mp"),
            P("seq", "mp"),
            P("seq", "mp"),
            P("mp", "seq"),
            P("seq"),
            P("seq", "mp"),
            P("seq", "mp"),
            P("mp", "seq"),
        ),
        check_vma=False,
    )
```

```python
import functools
import math

import jax
import jax.numpy as jnp
from jax import lax
from jax.experimental import pallas as pl
from jax.experimental.pallas import tpu as pltpu
from jax.sharding import PartitionSpec as P

HEAD_DIM = 128
WINDOW = 64
EPSILON = 1e-06
BF16 = jnp.bfloat16
F32 = jnp.float32
ANYWHERE = pl.BlockSpec(memory_space=pl.ANY)
HINT = 0.01


def cost(flops, bytes_accessed, transcendentals):
    return pl.CostEstimate(
        flops=int(HINT * flops),
        bytes_accessed=int(HINT * bytes_accessed),
        transcendentals=int(HINT * transcendentals),
    )


def mat_nn(left, right):
    return jnp.dot(left, right, preferred_element_type=F32)


def mat_nt(left, right):
    return lax.dot_general(left, right, (((1,), (1,)), ((), ())), preferred_element_type=F32)


def mat_tn(left, right):
    return lax.dot_general(left, right, (((0,), (0,)), ((), ())), preferred_element_type=F32)


def shift_pairs(count, steps):
    return [(s, s + steps) for s in range(max(0, -steps), min(count, count - steps))]


def flip_pairs(count, bit):
    return [(s, s ^ bit) for s in range(count)]


def relative_blocks(count):
    me = lax.axis_index("seq")
    place = jnp.arange(count, dtype=jnp.int32)
    outers = count // 4
    inner, middle, outer = place // (2 * outers), (place // outers) % 2, place % outers
    return (outer * 4 + ((me // 2 + middle) % 2) * 2 + (me + inner) % 2).astype(jnp.int32)


def rolled(values, steps, axis):
    return lax.dynamic_slice_in_dim(
        jnp.concatenate([values, values], axis), steps, values.shape[axis], axis
    )


def turn_blocks(pieces, order_ref, *refs):
    blocks = order_ref.shape[0] // 2
    first = 0
    for in_ref in refs[:pieces]:
        last = first + in_ref.shape[0]
        for half, out_ref in enumerate(refs[-2:]):
            for i in range(blocks):
                start = pl.multiple_of(order_ref[half * blocks + i] * 128, 128)
                out_ref[i * 128 : (i + 1) * 128, first:last] = in_ref[:, pl.ds(start, 128)].T
        first = last


def relative_turned(pieces, order, *after):
    rows, columns = sum(p.shape[0] for p in pieces), pieces[0].shape[1]
    count = order.shape[0]
    width = columns // count
    kind = pieces[0].dtype
    if width % 128:
        values = jnp.concatenate(pieces, 0)
        me, outers = lax.axis_index("seq"), count // 4
        turned = rolled(values.reshape(rows, outers, 2, 2, width), (me // 2) % 2, 2)
        turned = rolled(turned, me % 2, 3)
        return tuple(jnp.transpose(turned, (3, 2, 1, 4, 0)).reshape(2, columns // 2, rows))
    whole = pl.BlockSpec(memory_space=pltpu.VMEM)
    return pl.pallas_call(
        functools.partial(turn_blocks, len(pieces)),
        in_specs=[pl.BlockSpec(memory_space=pltpu.SMEM)] + [whole] * len(pieces) + [ANYWHERE] * len(after),
        out_specs=(whole, whole),
        out_shape=(jax.ShapeDtypeStruct((columns // 2, rows), kind),) * 2,
        cost_estimate=cost(flops=0, bytes_accessed=4 * rows * columns, transcendentals=0),
        compiler_params=pltpu.CompilerParams(vmem_limit_bytes=60 << 20),
    )(order, *pieces, *after)


def to_core(values):
    return lax.ppermute(values, "seq", flip_pairs(lax.axis_size("seq"), 1))


def to_middle(values):
    return lax.ppermute(values, "seq", flip_pairs(lax.axis_size("seq"), 2))


def sum_outer(values):
    outers = lax.axis_size("seq") // 4
    groups = [[o * 4 + place for o in range(outers)] for place in range(4)]
    return lax.psum_scatter(values, "seq", scatter_dimension=0, axis_index_groups=groups, tiled=True)


def sum_outer_direct(values):
    count = lax.axis_size("seq")
    outers = count // 4
    values = values.reshape(outers, values.shape[0] // outers, values.shape[1])
    outer = lax.axis_index("seq") // 4
    total = lax.dynamic_index_in_dim(values, outer, 0, keepdims=False).astype(F32)
    for step in range(1, outers):
        sent = lax.dynamic_index_in_dim(values, (outer + step) % outers, 0, keepdims=False)
        got = lax.ppermute(sent, "seq", [(s, (s + 4 * step) % count) for s in range(count)])
        total = total + got.astype(F32)
    return total


def add_block(keep_ref, got_ref, *refs):
    refs[-1][...] = (keep_ref[...].astype(F32) + got_ref[...].astype(F32)).astype(BF16)


def column_block(columns, most=1024):
    return next(w for w in range(most, 0, -128) if columns % w == 0)


def add_middle(part, after=()):
    keep, got = part[0], to_middle(part[1])
    rows, columns = keep.shape
    wide = column_block(columns)
    spec = pl.BlockSpec((rows, wide), lambda j: (0, j))
    return pl.pallas_call(
        add_block,
        grid=(columns // wide,),
        in_specs=[spec] * 2 + [ANYWHERE] * len(after),
        out_specs=spec,
        out_shape=jax.ShapeDtypeStruct((rows, columns), BF16),
        cost_estimate=cost(flops=rows * columns, bytes_accessed=6 * rows * columns, transcendentals=0),
        compiler_params=pltpu.CompilerParams(vmem_limit_bytes=60 << 20),
    )(keep, got, *after)


def sum_small(partial):
    count = lax.axis_size("seq")
    outers = count // 4
    rest = partial.shape[1:]
    partial = partial.reshape((2, 2 * outers) + rest)
    pair = partial[0] + to_core(partial[1])
    pair = pair.reshape((2, outers) + rest)
    four = pair[0] + to_middle(pair[1])
    outer = lax.axis_index("seq") // 4
    total = lax.dynamic_index_in_dim(four, outer, 0, keepdims=False)
    for step in range(1, outers):
        sent = lax.dynamic_index_in_dim(four, (outer + step) % outers, 0, keepdims=False)
        total = total + lax.ppermute(sent, "seq", [(s, (s + 4 * step) % count) for s in range(count)])
    return total


def bands(steps):
    return [
        (slice(i * WINDOW, (i + 1) * WINDOW), slice(i * WINDOW, (i + 2) * WINDOW)) for i in range(steps)
    ]


def band_probs(query, key, bias, steps):
    scale = 1.0 / math.sqrt(HEAD_DIM)
    scores = jnp.concatenate([mat_nt(query[rows], key[keys]) for rows, keys in bands(steps)], 0)
    scores = scores * scale + bias
    weights = jnp.exp(scores - jnp.max(scores, axis=1, keepdims=True))
    return weights / jnp.sum(weights, axis=1, keepdims=True)


def attend(q_ref, k_ref, v_ref, k_tail_ref, v_tail_ref, bias_ref, out_ref):
    steps = q_ref.shape[0] // WINDOW
    key = jnp.concatenate([k_tail_ref[...], k_ref[...]], 0)
    value = jnp.concatenate([v_tail_ref[...], v_ref[...]], 0)
    probs = band_probs(q_ref[...], key, bias_ref[...], steps).astype(BF16)
    for rows, keys in bands(steps):
        out_ref[rows] = mat_nn(probs[rows], value[keys]).astype(BF16)


def attend_back(heads, pieces, q_ref, k_ref, v_ref, k_tail_ref, v_tail_ref, bias_ref, *refs):
    q_next_ref, k_next_ref, v_next_ref = refs[:3]
    dq_ref, dkv_ref = refs[-2:]
    da = jnp.concatenate([r[...] for r in refs[3 : 4 + pieces]], 0)
    scale = 1.0 / math.sqrt(HEAD_DIM)
    head = pl.program_id(0)
    steps = da.shape[0] // WINDOW
    query = jnp.concatenate([q_ref[...], q_next_ref[...]], 0)
    key = jnp.concatenate([k_tail_ref[...], k_ref[...], k_next_ref[...]], 0)
    value = jnp.concatenate([v_tail_ref[...], v_ref[...], v_next_ref[...]], 0)
    probs = band_probs(query, key, bias_ref[...], steps)
    dp = jnp.concatenate([mat_nt(da[rows], value[keys]) for rows, keys in bands(steps)], 0)
    inner = jnp.sum(probs * dp, axis=1, keepdims=True)
    ds = (probs * (dp - inner)).astype(BF16)
    probs = probs.astype(BF16)
    low = None
    for i, (rows, keys) in enumerate(bands(steps)):
        if i < steps - 1:
            dq_ref[rows] = (mat_nn(ds[rows], key[keys]) * scale).astype(BF16)
        both = (mat_tn(ds[rows], query[rows]) * scale, mat_tn(probs[rows], da[rows]))
        if i:
            for part in range(2):
                columns = pl.ds(pl.multiple_of((part * heads + head) * HEAD_DIM, HEAD_DIM), HEAD_DIM)
                own_rows = slice((i - 1) * WINDOW, i * WINDOW)
                dkv_ref[own_rows, columns] = (both[part][:WINDOW] + low[part]).astype(BF16)
        low = [b[WINDOW:] for b in both]


def head_spec(rows, first=0):
    return pl.BlockSpec((rows, HEAD_DIM), lambda h: (0, first + h))


def once(shape):
    return pl.BlockSpec(shape, lambda j: (0, 0), pipeline_mode=pl.Buffered(1))


def attention_specs(tokens, heads, extra=0):
    return [
        head_spec(tokens),
        head_spec(tokens, heads),
        head_spec(tokens, 2 * heads),
        head_spec(WINDOW),
        head_spec(WINDOW, heads),
        once((tokens + extra, 2 * WINDOW)),
    ]


def attention_forward(qkv, tail, bias):
    tokens, heads = qkv.shape[0], qkv.shape[1] // (3 * HEAD_DIM)
    width = heads * HEAD_DIM
    return pl.pallas_call(
        attend,
        grid=(heads,),
        in_specs=attention_specs(tokens, heads),
        out_specs=head_spec(tokens),
        out_shape=jax.ShapeDtypeStruct((tokens, width), BF16),
        cost_estimate=cost(
            flops=8 * tokens * width * WINDOW, bytes_accessed=8 * tokens * width, transcendentals=tokens * width
        ),
        compiler_params=pltpu.CompilerParams(vmem_limit_bytes=60 << 20),
    )(qkv, qkv, qkv, tail, tail, bias)


def attention_backward(qkv, tail, bias, following, da, *after):
    tokens, heads = qkv.shape[0], qkv.shape[1] // (3 * HEAD_DIM)
    width = heads * HEAD_DIM
    return pl.pallas_call(
        functools.partial(attend_back, heads, len(da) - 1),
        grid=(heads,),
        in_specs=attention_specs(tokens, heads, WINDOW)
        + [head_spec(WINDOW, part * heads) for part in range(3)]
        + [head_spec(d.shape[0]) for d in da]
        + [ANYWHERE] * len(after),
        out_specs=(head_spec(tokens), once((tokens, 2 * width))),
        out_shape=(
            jax.ShapeDtypeStruct((tokens, width), BF16),
            jax.ShapeDtypeStruct((tokens, 2 * width), BF16),
        ),
        cost_estimate=cost(
            flops=20 * tokens * width * WINDOW, bytes_accessed=14 * tokens * width, transcendentals=tokens * width
        ),
        compiler_params=pltpu.CompilerParams(vmem_limit_bytes=60 << 20),
    )(qkv, qkv, qkv, tail, tail, bias, following, following, following, *da, *after)


def multiply(turned, pieces, *refs):
    w_ref = refs[pieces]
    total, first = None, 0
    for x_ref in refs[:pieces]:
        last = first + x_ref.shape[1]
        term = mat_nt(x_ref[...], w_ref[:, first:last]) if turned else mat_nn(x_ref[...], w_ref[...])
        total = term if total is None else total + term
        first = last
    refs[-1][...] = total.astype(BF16)


def rows_times(pieces, weights, columns, first=0, turned=False, wide=512, after=()):
    tokens, d = pieces[0].shape[0], sum(p.shape[1] for p in pieces)
    if turned:
        out = weights.shape[0]
        spec = pl.BlockSpec((wide, columns), lambda j: (j, first // columns))
    else:
        out = columns
        spec = pl.BlockSpec((d, wide), lambda j: (0, first // wide + j))
    return pl.pallas_call(
        functools.partial(multiply, turned, len(pieces)),
        grid=(out // wide,),
        in_specs=[once(p.shape) for p in pieces] + [spec] + [ANYWHERE] * len(after),
        out_specs=pl.BlockSpec((tokens, wide), lambda j: (0, j)),
        out_shape=jax.ShapeDtypeStruct((tokens, out), BF16),
        cost_estimate=cost(
            flops=2 * tokens * d * out, bytes_accessed=2 * (tokens * (d + out) + d * out), transcendentals=0
        ),
        compiler_params=pltpu.CompilerParams(vmem_limit_bytes=60 << 20),
    )(*pieces, weights, *after)


PARTS = ((768, 2), (640, 2))


def feed(block, steps, first_row, h_ref, dm_ref, wgu_ref, wd_ref, *refs):
    j = pl.program_id(0)
    carried = first_row is not None
    if carried:
        m_in, dh_in = refs[:2]
        wide_ref, hidden_ref, m_out, dh_out, m_sum, dh_sum, m_sem, dh_sem = refs[-8:]
        here = pl.ds(first_row, m_sum.shape[0])
        copies = (
            pltpu.make_async_copy(m_in.at[here], m_sum, m_sem),
            pltpu.make_async_copy(dh_in.at[here], dh_sum, dh_sem),
        )

        @pl.when(j == 0)
        def _():
            for copy in copies:
                copy.start()

    else:
        wide_ref, hidden_ref, m_sum, dh_sum = refs[-4:]
    taken = slice(first_row or 0, (first_row or 0) + m_sum.shape[0])
    gate_up = mat_nn(h_ref[taken], wgu_ref[...])
    gate, up = gate_up[:, :block], gate_up[:, block:]
    dhidden = mat_nn(dm_ref[taken], wd_ref[...])
    sigma = jax.nn.sigmoid(gate)
    silu = gate * sigma
    hidden = (silu * up).astype(BF16)
    dup = (dhidden * silu).astype(BF16)
    dgate = (dhidden * up * (sigma * (1.0 + gate * (1.0 - sigma)))).astype(BF16)
    dgate_up = jnp.concatenate([dgate, dup], 1)
    wide_ref[...] = dgate_up
    hidden_ref[...] = hidden

    @pl.when(j == 0)
    def _():
        if carried:
            for copy in copies:
                copy.wait()
        else:
            m_sum[...] = jnp.zeros_like(m_sum)
            dh_sum[...] = jnp.zeros_like(dh_sum)

    width = 512
    for c in range(0, m_sum.shape[1], width):
        part = slice(c, c + width)
        dh_sum[:, part] += mat_nt(dgate_up, wgu_ref[part])
        m_sum[:, part] += mat_nt(hidden, wd_ref[part])

    if carried:

        @pl.when(j == steps - 1)
        def _():
            m_out[...] = m_sum[...].astype(BF16)
            dh_out[...] = dh_sum[...].astype(BF16)


def feed_forward(rows, dm, weights, part, carry=(), place=0, count=1, after=()):
    d = rows.shape[1]
    block, steps = part
    wide = steps * block
    carried = bool(carry)
    tokens = count * 128 if carried else rows.shape[0]
    row_spec = once((tokens, d))
    kind = BF16 if carried else F32
    return pl.pallas_call(
        functools.partial(feed, block, steps, place * 128 if carried else None),
        grid=(steps,),
        in_specs=[
            once(rows.shape),
            once(rows.shape),
            pl.BlockSpec((d, 2 * block), lambda j: (0, j)),
            pl.BlockSpec((d, block), lambda j: (0, 2 * steps + j)),
        ]
        + [ANYWHERE] * (len(carry) + len(after)),
        out_specs=(
            pl.BlockSpec((tokens, 2 * block), lambda j: (0, j)),
            pl.BlockSpec((tokens, block), lambda j: (0, j)),
            row_spec,
            row_spec,
        ),
        out_shape=(
            jax.ShapeDtypeStruct((tokens, 2 * wide), BF16),
            jax.ShapeDtypeStruct((tokens, wide), BF16),
            jax.ShapeDtypeStruct((tokens, d), kind),
            jax.ShapeDtypeStruct((tokens, d), kind),
        ),
        scratch_shapes=([pltpu.VMEM((tokens, d), F32)] * 2 + [pltpu.SemaphoreType.DMA] * 2) if carried else [],
        cost_estimate=cost(
            flops=12 * tokens * d * wide, bytes_accessed=6 * d * wide + 24 * tokens * d, transcendentals=tokens * wide
        ),
        compiler_params=pltpu.CompilerParams(vmem_limit_bytes=60 << 20),
    )(rows, dm, weights, weights, *carry, *after)


def grad_block(pieces, outers, left_ref, left_got_ref, *refs):
    keep_ref, send_ref = refs[-2:]
    total = None
    for side, left in enumerate((left_ref, left_got_ref)):
        first = 0
        for right in refs[side * pieces : (side + 1) * pieces]:
            last = first + right.shape[0]
            term = mat_nn(left[:, first:last], right[...])
            total = term if total is None else total + term
            first = last
    total = total.astype(BF16)
    half = total.shape[0] // 2
    if not outers:
        keep_ref[...] = total[:half]
        send_ref[...] = total[half:]
        return
    block = half // outers
    for i in range(2 * outers):
        first = (i % 2) * half + (i // 2) * block
        send_ref[i * block : (i + 1) * block] = total[first : first + block]


def weight_grad(left, right, after=(), first=0, columns=None, outers=0):
    d, tokens = left[0].shape
    columns = columns or right[0][0].shape[1]
    wide = next(w for w in (640, 512, 256, 128) if columns % w == 0 and first % w == 0)
    pieces = tuple(right[0]) + tuple(right[1])
    outs = (jax.ShapeDtypeStruct((d, columns), BF16),)
    if not outers:
        outs = (jax.ShapeDtypeStruct((d // 2, columns), BF16),) * 2
    return pl.pallas_call(
        functools.partial(grad_block, len(right[0]), outers),
        grid=(columns // wide,),
        in_specs=[once((d, tokens))] * 2
        + [pl.BlockSpec((p.shape[0], wide), lambda j: (0, first // wide + j)) for p in pieces]
        + [ANYWHERE] * len(after),
        out_specs=(pl.BlockSpec((d // len(outs), wide), lambda j: (0, j)),) * len(outs),
        out_shape=outs,
        cost_estimate=cost(
            flops=4 * tokens * d * columns, bytes_accessed=2 * (d + 2 * tokens) * columns + 4 * d * tokens, transcendentals=0
        ),
        compiler_params=pltpu.CompilerParams(vmem_limit_bytes=60 << 20),
    )(*left, *pieces, *after)


def middle_back(own_ref, got_ref, middle_ref, dm_ref, gain_ref, wo_ref, *refs):
    grad_ref, low_ref, da_ref, gain_out = refs[-4:]
    rows = middle_ref[...]
    inverse = lax.rsqrt(jnp.mean(rows * rows, axis=1, keepdims=True) + EPSILON)
    unit = rows * inverse
    dh = own_ref[...].astype(F32) + got_ref[...].astype(F32)
    grad = dm_ref[...].astype(F32) + norm_back(dh, unit, inverse, gain_ref[...])
    grad_ref[...] = grad
    low = grad.astype(BF16)
    low_ref[...] = low
    da_ref[...] = mat_nn(low, wo_ref[...]).astype(BF16)
    part = jnp.sum(dh * unit, axis=0, keepdims=True)

    @pl.when(pl.program_id(0) == 0)
    def _():
        gain_out[...] = part

    @pl.when(pl.program_id(0) > 0)
    def _():
        gain_out[...] += part


def middle_gradient(own, got, middle, dm, gain, weights, width, place, after=()):
    tokens, d = own.shape

    def rows(first, n=d):
        return pl.BlockSpec((128, n), lambda i: (first + i, 0))

    return pl.pallas_call(
        middle_back,
        grid=(tokens // 128,),
        in_specs=[
            rows(0),
            rows(0),
            rows(place),
            rows(place),
            once((1, d)),
            pl.BlockSpec((d, width), lambda i: (0, 3), pipeline_mode=pl.Buffered(1)),
        ]
        + [ANYWHERE] * len(after),
        out_specs=(rows(0), rows(0), rows(0, width), once((1, d))),
        out_shape=(
            jax.ShapeDtypeStruct((tokens, d), F32),
            jax.ShapeDtypeStruct((tokens, d), BF16),
            jax.ShapeDtypeStruct((tokens, width), BF16),
            jax.ShapeDtypeStruct((1, d), F32),
        ),
        cost_estimate=cost(
            flops=2 * tokens * d * width, bytes_accessed=2 * d * width + 16 * tokens * d, transcendentals=0
        ),
        compiler_params=pltpu.CompilerParams(vmem_limit_bytes=60 << 20),
    )(own, got, middle, dm, gain, weights, *after)


def norm_back(grad_normed, unit_rows, inverse_rows, gain):
    scaled = grad_normed * gain
    return inverse_rows * (scaled - unit_rows * jnp.mean(scaled * unit_rows, axis=1, keepdims=True))


def gather(shards):
    return lax.all_gather(jnp.concatenate(shards, 1), "seq", axis=0, tiled=True)


def per_device(
    x_in, lengths, g_attn, w_query, w_key, w_value, w_out, g_ffn, w_gate, w_up, w_down, cotangent
):
    tokens = x_in.shape[0]
    width = w_query.shape[1]
    ff = w_gate.shape[1]
    count = lax.axis_size("seq")
    def rounded(shard, a=0, b=None):
        shard = shard.astype(BF16)
        b = shard.shape[1] if b is None else b
        pad = max(0, b - shard.shape[1])
        return jnp.pad(shard[:, a:b], ((0, 0), (0, pad)))

    def zeros(n):
        return jnp.zeros((w_query.shape[0], n), BF16)

    w_down_t = w_down.astype(BF16).T
    gains_here = rounded(jnp.stack([g_attn, g_ffn], 1), 0, 128)
    attn_w = gather(
        (rounded(w_query), rounded(w_key), rounded(w_value), w_out.astype(BF16).T, gains_here)
    )
    ffn_w = []
    a = 0
    for block, steps in PARTS:
        wide = [rounded(w, a + j * block, a + (j + 1) * block) for j in range(steps) for w in (w_gate, w_up)]
        wide.append(rounded(w_down_t, a, a + steps * block))
        spare = 4224 - 3 * steps * block
        ffn_w.append(gather(wide + ([zeros(spare)] if spare > 0 else [])))
        a += steps * block
    gains = attn_w[:, 4 * width : 4 * width + 2].T.astype(F32)
    gain_one, gain_two = gains[0], gains[1]

    order = relative_blocks(count)
    first_place = lax.axis_index("seq") * tokens
    row = jnp.arange(tokens + WINDOW, dtype=jnp.int32)[:, None]
    column = jnp.arange(2 * WINDOW, dtype=jnp.int32)[None, :]
    key_place = row // WINDOW * WINDOW + column - WINDOW
    ends = [lengths[0]]
    for i in range(1, lengths.shape[0] - 1):
        ends.append(ends[-1] + lengths[i])
    seg_row = sum(((first_place + row) >= e).astype(jnp.int32) for e in ends)
    seg_key = sum(((first_place + key_place) >= e).astype(jnp.int32) for e in ends)
    allowed = (
        (key_place <= row)
        & (key_place > row - WINDOW)
        & (first_place + key_place >= 0)
        & (seg_row == seg_key)
    )
    bias = jnp.where(allowed, 0.0, -1e30).astype(F32)

    x_full = x_in.astype(F32)
    inverse_one = lax.rsqrt(jnp.mean(x_full * x_full, axis=1, keepdims=True) + EPSILON)
    unit_one = x_full * inverse_one
    def both_halves(pieces, *after):
        own, other = relative_turned(pieces, order, *after)
        return own, to_core(other)

    def both_cores(*pieces):
        return pieces, tuple(to_core(p) for p in pieces)

    def to_mp(own):
        return lax.ppermute(own, "mp", [(0, 1), (1, 0)])

    cot_turned = both_halves((cotangent,))
    normed = (unit_one * gain_one).astype(BF16)
    normed_turned = both_halves((normed,))

    qkv = rows_times((normed,), attn_w, 3 * width)
    tail = lax.ppermute(qkv[tokens - WINDOW :, width:], "seq", shift_pairs(count, 1))
    following = lax.ppermute(qkv[:WINDOW], "seq", shift_pairs(count, -1))
    mixed = attention_forward(qkv, tail, bias[:tokens])
    mixed_both = both_cores(mixed)
    branch = rows_times((mixed,), attn_w, width, 3 * width, True)
    middle = x_full + (branch.astype(F32) + to_mp(branch).astype(F32))
    inverse_two = lax.rsqrt(jnp.mean(middle * middle, axis=1, keepdims=True) + EPSILON)
    normed_two = (middle * inverse_two * gain_two).astype(BF16)
    normed_two_turned = both_halves((normed_two,))

    after = (mixed_both[1][0], cot_turned[1], normed_turned[1], following)
    one, two = (block * steps for block, steps in PARTS)
    wide_acts, hidden, *carry = feed_forward(normed_two, cotangent, ffn_w[0], PARTS[0], after=after)
    wide_acts = both_cores(wide_acts)
    one_a = weight_grad(normed_two_turned, wide_acts, (), 0, one)
    one_c = weight_grad(cot_turned, both_cores(hidden), one_a, outers=count // 4)
    one_b = weight_grad(normed_two_turned, wide_acts, one_c, one, one)
    one_c = sum_outer(one_c[0])
    places = ((0, (tokens // 128 + 1) // 2), ((tokens // 128 + 1) // 2, tokens // 256))
    after = one_b
    halves = []
    for place, blocks in places:
        halves.append(feed_forward(normed_two, cotangent, ffn_w[1], PARTS[1], tuple(carry), place, blocks, after))
        if not place:
            one_a = add_middle(one_a, (halves[0][0],))
            after = (one_a,)
    wide_acts, hidden, m_halves, dh_halves = zip(*halves)
    after = (wide_acts[1],)
    wide_acts, hidden = both_cores(*wide_acts), both_cores(*hidden)
    half = one_c.shape[0] // 2
    one_c = one_c[:half].astype(F32) + to_middle(one_c[half:]).astype(F32)
    middles = []
    for (place, _), dh in zip(places, dh_halves):
        middles.append(
            middle_gradient(dh, to_mp(dh), middle, cotangent, gain_two[None], attn_w, width, place, after)
        )
        if not place:
            two_a = weight_grad(normed_two_turned, wide_acts, (middles[0][1],), 0, two)
            da_next = lax.ppermute(middles[0][2][:WINDOW], "seq", shift_pairs(count, -1))
            after = (*two_a, da_next, one_c)
    grad_gain_two = sum(m[3][0] for m in middles)
    one_b = add_middle(one_b, (middles[1][1],))
    two_b = weight_grad(normed_two_turned, wide_acts, (one_b,), two, two)
    one_a, one_b = sum_outer(one_a), sum_outer(one_b)
    branch_turned = both_halves([m[1] for m in middles], *two_b)
    da = [m[2] for m in middles] + [da_next]
    grad_q, grad_kv = attention_backward(qkv, tail, bias, following, da, branch_turned[0])
    two_a = add_middle(two_a, (grad_q, one_a))
    two_c = weight_grad(cot_turned, hidden, (two_a,))
    two_b = add_middle(two_b, two_c)
    after = (two_b,)
    two_a, two_b = sum_outer(two_a), sum_outer(two_b)
    late, _ = lax.optimization_barrier((m_halves, branch_turned[0]))
    late = jnp.concatenate(late, 0)
    late_got = to_mp(late)
    q_part = weight_grad(normed_turned, both_cores(grad_q), after)
    kv_part = weight_grad(normed_turned, both_cores(grad_kv), (*q_part, one_b))
    own = rows_times((grad_q, grad_kv), attn_w, 3 * width, 0, True, after=kv_part)
    own_got = to_mp(own)
    out_part = weight_grad(branch_turned, mixed_both, (own, two_a))
    two_c = add_middle(two_c, (*out_part, late_got))
    q_part = add_middle(q_part, (two_c,))
    mixed_sum = sum_outer(jnp.concatenate([two_c, q_part], 1))
    down_two, q_sum = mixed_sum[:, :two], mixed_sum[:, two:].astype(F32)
    kv_part = add_middle(kv_part, (q_part, two_b, own_got))
    kv_sum = sum_outer(kv_part).astype(F32)
    out_part = add_middle(out_part, (kv_part, mixed_sum))
    out_sum = sum_outer_direct(out_part)
    grad_normed = own.astype(F32) + own_got.astype(F32)
    grad_gain_one = jnp.sum(own.astype(F32) * unit_one, axis=0)
    grad_gain_one = grad_gain_one + to_mp(grad_gain_one)
    grad_middle = jnp.concatenate([m[0] for m in middles], 0)
    grad_input = grad_middle + norm_back(grad_normed, unit_one, inverse_one, gain_one)
    result = middle + (late.astype(F32) + late_got.astype(F32))
    gain_parts = jnp.stack([grad_gain_one, grad_gain_two], 0)
    gain_blocks = jnp.swapaxes(gain_parts.reshape(2, count, -1), 0, 1)
    chosen = order[:, None] == jnp.arange(count, dtype=jnp.int32)[None, :]
    gain_rel = jnp.sum(jnp.where(chosen[:, :, None, None], gain_blocks[None], 0.0), axis=1)
    gain_sums = sum_small(gain_rel)

    wide_one, wide_two = jnp.concatenate([one_a, one_b], 1), jnp.concatenate([two_a, two_b], 1)

    def columns(which):
        pieces = []
        for (block, steps), wide in zip(PARTS, (wide_one, wide_two)):
            pieces += [wide[:, (2 * j + which) * block : (2 * j + which + 1) * block] for j in range(steps)]
        return jnp.concatenate(pieces, 1)[:, :ff].astype(F32)

    grad_gate, grad_up = columns(0), columns(1)
    grad_down = jnp.concatenate([one_c, down_two.astype(F32)], 1)[:, :ff].astype(F32)

    return (
        result.astype(BF16),
        grad_input.astype(BF16),
        gain_sums[0],
        q_sum,
        kv_sum[:, :width],
        kv_sum[:, width:],
        out_sum.T,
        gain_sums[1],
        grad_gate,
        grad_up,
        grad_down.T,
    )


def solution(mesh):
    placed = (
        P("seq", None),
        P(),
        P("seq"),
        P("seq", "mp"),
        P("seq", "mp"),
        P("seq", "mp"),
        P("mp", "seq"),
        P("seq"),
        P("seq", "mp"),
        P("seq", "mp"),
        P("mp", "seq"),
        P("seq", None),
    )
    return jax.shard_map(
        per_device,
        mesh=mesh,
        in_specs=placed,
        out_specs=(
            P("seq", None),
            P("seq", None),
            P("seq"),
            P("seq", "mp"),
            P("seq", "mp"),
            P("seq", "mp"),
            P("mp", "seq"),
            P("seq"),
            P("seq", "mp"),
            P("seq", "mp"),
            P("mp", "seq"),
        ),
        check_vma=False,
    )
```

```python
import functools
import math

import jax
import jax.numpy as jnp
from jax import lax
from jax.experimental import pallas as pl
from jax.experimental.pallas import tpu as pltpu
from jax.sharding import PartitionSpec as P

HEAD_DIM = 128
WINDOW = 64
EPSILON = 1e-06
BF16 = jnp.bfloat16
F32 = jnp.float32
ANYWHERE = pl.BlockSpec(memory_space=pl.ANY)
HINT = 0.01


def cost(flops, bytes_accessed, transcendentals):
    return pl.CostEstimate(
        flops=int(HINT * flops),
        bytes_accessed=int(HINT * bytes_accessed),
        transcendentals=int(HINT * transcendentals),
    )


def mat_nn(left, right):
    return jnp.dot(left, right, preferred_element_type=F32)


def mat_nt(left, right):
    return lax.dot_general(left, right, (((1,), (1,)), ((), ())), preferred_element_type=F32)


def mat_tn(left, right):
    return lax.dot_general(left, right, (((0,), (0,)), ((), ())), preferred_element_type=F32)


def shift_pairs(count, steps):
    return [(s, s + steps) for s in range(max(0, -steps), min(count, count - steps))]


def flip_pairs(count, bit):
    return [(s, s ^ bit) for s in range(count)]


def relative_blocks(count):
    me = lax.axis_index("seq")
    place = jnp.arange(count, dtype=jnp.int32)
    outers = count // 4
    inner, middle, outer = place // (2 * outers), (place // outers) % 2, place % outers
    return (outer * 4 + ((me // 2 + middle) % 2) * 2 + (me + inner) % 2).astype(jnp.int32)


def rolled(values, steps, axis):
    return lax.dynamic_slice_in_dim(
        jnp.concatenate([values, values], axis), steps, values.shape[axis], axis
    )


def turn_blocks(pieces, order_ref, *refs):
    blocks = order_ref.shape[0] // 2
    first = 0
    for in_ref in refs[:pieces]:
        last = first + in_ref.shape[0]
        for half, out_ref in enumerate(refs[-2:]):
            for i in range(blocks):
                start = pl.multiple_of(order_ref[half * blocks + i] * 128, 128)
                out_ref[i * 128 : (i + 1) * 128, first:last] = in_ref[:, pl.ds(start, 128)].T
        first = last


def relative_turned(pieces, order, *after):
    rows, columns = sum(p.shape[0] for p in pieces), pieces[0].shape[1]
    count = order.shape[0]
    width = columns // count
    kind = pieces[0].dtype
    if width % 128:
        values = jnp.concatenate(pieces, 0)
        me, outers = lax.axis_index("seq"), count // 4
        turned = rolled(values.reshape(rows, outers, 2, 2, width), (me // 2) % 2, 2)
        turned = rolled(turned, me % 2, 3)
        return tuple(jnp.transpose(turned, (3, 2, 1, 4, 0)).reshape(2, columns // 2, rows))
    whole = pl.BlockSpec(memory_space=pltpu.VMEM)
    return pl.pallas_call(
        functools.partial(turn_blocks, len(pieces)),
        in_specs=[pl.BlockSpec(memory_space=pltpu.SMEM)] + [whole] * len(pieces) + [ANYWHERE] * len(after),
        out_specs=(whole, whole),
        out_shape=(jax.ShapeDtypeStruct((columns // 2, rows), kind),) * 2,
        cost_estimate=cost(flops=0, bytes_accessed=4 * rows * columns, transcendentals=0),
        compiler_params=pltpu.CompilerParams(vmem_limit_bytes=60 << 20),
    )(order, *pieces, *after)


def to_core(values):
    return lax.ppermute(values, "seq", flip_pairs(lax.axis_size("seq"), 1))


def to_middle(values):
    return lax.ppermute(values, "seq", flip_pairs(lax.axis_size("seq"), 2))


def sum_outer(values):
    outers = lax.axis_size("seq") // 4
    groups = [[o * 4 + place for o in range(outers)] for place in range(4)]
    return lax.psum_scatter(values, "seq", scatter_dimension=0, axis_index_groups=groups, tiled=True)


def sum_outer_direct(values):
    count = lax.axis_size("seq")
    outers = count // 4
    values = values.reshape(outers, values.shape[0] // outers, values.shape[1])
    outer = lax.axis_index("seq") // 4
    total = lax.dynamic_index_in_dim(values, outer, 0, keepdims=False).astype(F32)
    for step in range(1, outers):
        sent = lax.dynamic_index_in_dim(values, (outer + step) % outers, 0, keepdims=False)
        got = lax.ppermute(sent, "seq", [(s, (s + 4 * step) % count) for s in range(count)])
        total = total + got.astype(F32)
    return total


def add_block(keep_ref, got_ref, *refs):
    refs[-1][...] = (keep_ref[...].astype(F32) + got_ref[...].astype(F32)).astype(BF16)


def column_block(columns, most=1024):
    return next(w for w in range(most, 0, -128) if columns % w == 0)


def add_middle(part, after=()):
    keep, got = part[0], to_middle(part[1])
    rows, columns = keep.shape
    wide = column_block(columns)
    spec = pl.BlockSpec((rows, wide), lambda j: (0, j))
    return pl.pallas_call(
        add_block,
        grid=(columns // wide,),
        in_specs=[spec] * 2 + [ANYWHERE] * len(after),
        out_specs=spec,
        out_shape=jax.ShapeDtypeStruct((rows, columns), BF16),
        cost_estimate=cost(flops=rows * columns, bytes_accessed=6 * rows * columns, transcendentals=0),
        compiler_params=pltpu.CompilerParams(vmem_limit_bytes=60 << 20),
    )(keep, got, *after)


def sum_small(partial):
    count = lax.axis_size("seq")
    outers = count // 4
    rest = partial.shape[1:]
    partial = partial.reshape((2, 2 * outers) + rest)
    pair = partial[0] + to_core(partial[1])
    pair = pair.reshape((2, outers) + rest)
    four = pair[0] + to_middle(pair[1])
    outer = lax.axis_index("seq") // 4
    total = lax.dynamic_index_in_dim(four, outer, 0, keepdims=False)
    for step in range(1, outers):
        sent = lax.dynamic_index_in_dim(four, (outer + step) % outers, 0, keepdims=False)
        total = total + lax.ppermute(sent, "seq", [(s, (s + 4 * step) % count) for s in range(count)])
    return total


def bands(steps):
    return [
        (slice(i * WINDOW, (i + 1) * WINDOW), slice(i * WINDOW, (i + 2) * WINDOW)) for i in range(steps)
    ]


def band_probs(query, key, bias, steps):
    scale = 1.0 / math.sqrt(HEAD_DIM)
    scores = jnp.concatenate([mat_nt(query[rows], key[keys]) for rows, keys in bands(steps)], 0)
    scores = scores * scale + bias
    weights = jnp.exp(scores - jnp.max(scores, axis=1, keepdims=True))
    return weights / jnp.sum(weights, axis=1, keepdims=True)


def attend(q_ref, k_ref, v_ref, k_tail_ref, v_tail_ref, bias_ref, out_ref):
    steps = q_ref.shape[0] // WINDOW
    key = jnp.concatenate([k_tail_ref[...], k_ref[...]], 0)
    value = jnp.concatenate([v_tail_ref[...], v_ref[...]], 0)
    probs = band_probs(q_ref[...], key, bias_ref[...], steps).astype(BF16)
    for rows, keys in bands(steps):
        out_ref[rows] = mat_nn(probs[rows], value[keys]).astype(BF16)


def attend_back(heads, pieces, q_ref, k_ref, v_ref, k_tail_ref, v_tail_ref, bias_ref, *refs):
    q_next_ref, k_next_ref, v_next_ref = refs[:3]
    dq_ref, dkv_ref = refs[-2:]
    da = jnp.concatenate([r[...] for r in refs[3 : 4 + pieces]], 0)
    scale = 1.0 / math.sqrt(HEAD_DIM)
    head = pl.program_id(0)
    steps = da.shape[0] // WINDOW
    query = jnp.concatenate([q_ref[...], q_next_ref[...]], 0)
    key = jnp.concatenate([k_tail_ref[...], k_ref[...], k_next_ref[...]], 0)
    value = jnp.concatenate([v_tail_ref[...], v_ref[...], v_next_ref[...]], 0)
    probs = band_probs(query, key, bias_ref[...], steps)
    dp = jnp.concatenate([mat_nt(da[rows], value[keys]) for rows, keys in bands(steps)], 0)
    inner = jnp.sum(probs * dp, axis=1, keepdims=True)
    ds = (probs * (dp - inner)).astype(BF16)
    probs = probs.astype(BF16)
    low = None
    for i, (rows, keys) in enumerate(bands(steps)):
        if i < steps - 1:
            dq_ref[rows] = (mat_nn(ds[rows], key[keys]) * scale).astype(BF16)
        both = (mat_tn(ds[rows], query[rows]) * scale, mat_tn(probs[rows], da[rows]))
        if i:
            for part in range(2):
                columns = pl.ds(pl.multiple_of((part * heads + head) * HEAD_DIM, HEAD_DIM), HEAD_DIM)
                own_rows = slice((i - 1) * WINDOW, i * WINDOW)
                dkv_ref[own_rows, columns] = (both[part][:WINDOW] + low[part]).astype(BF16)
        low = [b[WINDOW:] for b in both]


def head_spec(rows, first=0):
    return pl.BlockSpec((rows, HEAD_DIM), lambda h: (0, first + h))


def once(shape):
    return pl.BlockSpec(shape, lambda j: (0, 0), pipeline_mode=pl.Buffered(1))


def attention_specs(tokens, heads, extra=0):
    return [
        head_spec(tokens),
        head_spec(tokens, heads),
        head_spec(tokens, 2 * heads),
        head_spec(WINDOW),
        head_spec(WINDOW, heads),
        once((tokens + extra, 2 * WINDOW)),
    ]


def attention_forward(qkv, tail, bias):
    tokens, heads = qkv.shape[0], qkv.shape[1] // (3 * HEAD_DIM)
    width = heads * HEAD_DIM
    return pl.pallas_call(
        attend,
        grid=(heads,),
        in_specs=attention_specs(tokens, heads),
        out_specs=head_spec(tokens),
        out_shape=jax.ShapeDtypeStruct((tokens, width), BF16),
        cost_estimate=cost(
            flops=8 * tokens * width * WINDOW, bytes_accessed=8 * tokens * width, transcendentals=tokens * width
        ),
        compiler_params=pltpu.CompilerParams(vmem_limit_bytes=60 << 20),
    )(qkv, qkv, qkv, tail, tail, bias)


def attention_backward(qkv, tail, bias, following, da, *after):
    tokens, heads = qkv.shape[0], qkv.shape[1] // (3 * HEAD_DIM)
    width = heads * HEAD_DIM
    return pl.pallas_call(
        functools.partial(attend_back, heads, len(da) - 1),
        grid=(heads,),
        in_specs=attention_specs(tokens, heads, WINDOW)
        + [head_spec(WINDOW, part * heads) for part in range(3)]
        + [head_spec(d.shape[0]) for d in da]
        + [ANYWHERE] * len(after),
        out_specs=(head_spec(tokens), once((tokens, 2 * width))),
        out_shape=(
            jax.ShapeDtypeStruct((tokens, width), BF16),
            jax.ShapeDtypeStruct((tokens, 2 * width), BF16),
        ),
        cost_estimate=cost(
            flops=20 * tokens * width * WINDOW, bytes_accessed=14 * tokens * width, transcendentals=tokens * width
        ),
        compiler_params=pltpu.CompilerParams(vmem_limit_bytes=60 << 20),
    )(qkv, qkv, qkv, tail, tail, bias, following, following, following, *da, *after)


def multiply(turned, pieces, *refs):
    w_ref = refs[pieces]
    total, first = None, 0
    for x_ref in refs[:pieces]:
        last = first + x_ref.shape[1]
        term = mat_nt(x_ref[...], w_ref[:, first:last]) if turned else mat_nn(x_ref[...], w_ref[...])
        total = term if total is None else total + term
        first = last
    refs[-1][...] = total.astype(BF16)


def rows_times(pieces, weights, columns, first=0, turned=False, wide=512, after=()):
    tokens, d = pieces[0].shape[0], sum(p.shape[1] for p in pieces)
    if turned:
        out = weights.shape[0]
        spec = pl.BlockSpec((wide, columns), lambda j: (j, first // columns))
    else:
        out = columns
        spec = pl.BlockSpec((d, wide), lambda j: (0, first // wide + j))
    return pl.pallas_call(
        functools.partial(multiply, turned, len(pieces)),
        grid=(out // wide,),
        in_specs=[once(p.shape) for p in pieces] + [spec] + [ANYWHERE] * len(after),
        out_specs=pl.BlockSpec((tokens, wide), lambda j: (0, j)),
        out_shape=jax.ShapeDtypeStruct((tokens, out), BF16),
        cost_estimate=cost(
            flops=2 * tokens * d * out, bytes_accessed=2 * (tokens * (d + out) + d * out), transcendentals=0
        ),
        compiler_params=pltpu.CompilerParams(vmem_limit_bytes=60 << 20),
    )(*pieces, weights, *after)


PARTS = ((768, 2), (640, 2))


def feed(block, steps, first_row, h_ref, dm_ref, wgu_ref, wd_ref, *refs):
    j = pl.program_id(0)
    carried = first_row is not None
    if carried:
        m_in, dh_in = refs[:2]
        wide_ref, hidden_ref, m_out, dh_out, m_sum, dh_sum, m_sem, dh_sem = refs[-8:]
        here = pl.ds(first_row, m_sum.shape[0])
        copies = (
            pltpu.make_async_copy(m_in.at[here], m_sum, m_sem),
            pltpu.make_async_copy(dh_in.at[here], dh_sum, dh_sem),
        )

        @pl.when(j == 0)
        def _():
            for copy in copies:
                copy.start()

    else:
        wide_ref, hidden_ref, m_sum, dh_sum = refs[-4:]
    taken = slice(first_row or 0, (first_row or 0) + m_sum.shape[0])
    gate_up = mat_nn(h_ref[taken], wgu_ref[...])
    gate, up = gate_up[:, :block], gate_up[:, block:]
    dhidden = mat_nn(dm_ref[taken], wd_ref[...])
    sigma = jax.nn.sigmoid(gate)
    silu = gate * sigma
    hidden = (silu * up).astype(BF16)
    dup = (dhidden * silu).astype(BF16)
    dgate = (dhidden * up * (sigma * (1.0 + gate * (1.0 - sigma)))).astype(BF16)
    dgate_up = jnp.concatenate([dgate, dup], 1)
    wide_ref[...] = dgate_up
    hidden_ref[...] = hidden

    @pl.when(j == 0)
    def _():
        if carried:
            for copy in copies:
                copy.wait()
        else:
            m_sum[...] = jnp.zeros_like(m_sum)
            dh_sum[...] = jnp.zeros_like(dh_sum)

    width = 512
    for c in range(0, m_sum.shape[1], width):
        part = slice(c, c + width)
        dh_sum[:, part] += mat_nt(dgate_up, wgu_ref[part])
        m_sum[:, part] += mat_nt(hidden, wd_ref[part])

    if carried:

        @pl.when(j == steps - 1)
        def _():
            m_out[...] = m_sum[...].astype(BF16)
            dh_out[...] = dh_sum[...].astype(BF16)


def feed_forward(rows, dm, weights, part, carry=(), place=0, count=1, after=()):
    d = rows.shape[1]
    block, steps = part
    wide = steps * block
    carried = bool(carry)
    tokens = count * 128 if carried else rows.shape[0]
    row_spec = once((tokens, d))
    kind = BF16 if carried else F32
    return pl.pallas_call(
        functools.partial(feed, block, steps, place * 128 if carried else None),
        grid=(steps,),
        in_specs=[
            once(rows.shape),
            once(rows.shape),
            pl.BlockSpec((d, 2 * block), lambda j: (0, j)),
            pl.BlockSpec((d, block), lambda j: (0, 2 * steps + j)),
        ]
        + [ANYWHERE] * (len(carry) + len(after)),
        out_specs=(
            pl.BlockSpec((tokens, 2 * block), lambda j: (0, j)),
            pl.BlockSpec((tokens, block), lambda j: (0, j)),
            row_spec,
            row_spec,
        ),
        out_shape=(
            jax.ShapeDtypeStruct((tokens, 2 * wide), BF16),
            jax.ShapeDtypeStruct((tokens, wide), BF16),
            jax.ShapeDtypeStruct((tokens, d), kind),
            jax.ShapeDtypeStruct((tokens, d), kind),
        ),
        scratch_shapes=([pltpu.VMEM((tokens, d), F32)] * 2 + [pltpu.SemaphoreType.DMA] * 2) if carried else [],
        cost_estimate=cost(
            flops=12 * tokens * d * wide, bytes_accessed=6 * d * wide + 24 * tokens * d, transcendentals=tokens * wide
        ),
        compiler_params=pltpu.CompilerParams(vmem_limit_bytes=60 << 20),
    )(rows, dm, weights, weights, *carry, *after)


def grad_block(pieces, outers, left_ref, left_got_ref, *refs):
    keep_ref, send_ref = refs[-2:]
    total = None
    for side, left in enumerate((left_ref, left_got_ref)):
        first = 0
        for right in refs[side * pieces : (side + 1) * pieces]:
            last = first + right.shape[0]
            term = mat_nn(left[:, first:last], right[...])
            total = term if total is None else total + term
            first = last
    total = total.astype(BF16)
    half = total.shape[0] // 2
    if not outers:
        keep_ref[...] = total[:half]
        send_ref[...] = total[half:]
        return
    block = half // outers
    for i in range(2 * outers):
        first = (i % 2) * half + (i // 2) * block
        send_ref[i * block : (i + 1) * block] = total[first : first + block]


def weight_grad(left, right, after=(), first=0, columns=None, outers=0):
    d, tokens = left[0].shape
    columns = columns or right[0][0].shape[1]
    wide = next(w for w in (640, 512, 256, 128) if columns % w == 0 and first % w == 0)
    pieces = tuple(right[0]) + tuple(right[1])
    outs = (jax.ShapeDtypeStruct((d, columns), BF16),)
    if not outers:
        outs = (jax.ShapeDtypeStruct((d // 2, columns), BF16),) * 2
    return pl.pallas_call(
        functools.partial(grad_block, len(right[0]), outers),
        grid=(columns // wide,),
        in_specs=[once((d, tokens))] * 2
        + [pl.BlockSpec((p.shape[0], wide), lambda j: (0, first // wide + j)) for p in pieces]
        + [ANYWHERE] * len(after),
        out_specs=(pl.BlockSpec((d // len(outs), wide), lambda j: (0, j)),) * len(outs),
        out_shape=outs,
        cost_estimate=cost(
            flops=4 * tokens * d * columns, bytes_accessed=2 * (d + 2 * tokens) * columns + 4 * d * tokens, transcendentals=0
        ),
        compiler_params=pltpu.CompilerParams(vmem_limit_bytes=60 << 20),
    )(*left, *pieces, *after)


def middle_back(own_ref, got_ref, middle_ref, dm_ref, gain_ref, wo_ref, *refs):
    grad_ref, low_ref, da_ref, gain_out = refs[-4:]
    rows = middle_ref[...]
    inverse = lax.rsqrt(jnp.mean(rows * rows, axis=1, keepdims=True) + EPSILON)
    unit = rows * inverse
    dh = own_ref[...].astype(F32) + got_ref[...].astype(F32)
    grad = dm_ref[...].astype(F32) + norm_back(dh, unit, inverse, gain_ref[...])
    grad_ref[...] = grad
    low = grad.astype(BF16)
    low_ref[...] = low
    da_ref[...] = mat_nn(low, wo_ref[...]).astype(BF16)
    part = jnp.sum(dh * unit, axis=0, keepdims=True)

    @pl.when(pl.program_id(0) == 0)
    def _():
        gain_out[...] = part

    @pl.when(pl.program_id(0) > 0)
    def _():
        gain_out[...] += part


def middle_gradient(own, got, middle, dm, gain, weights, width, place, after=()):
    tokens, d = own.shape

    def rows(first, n=d):
        return pl.BlockSpec((128, n), lambda i: (first + i, 0))

    return pl.pallas_call(
        middle_back,
        grid=(tokens // 128,),
        in_specs=[
            rows(0),
            rows(0),
            rows(place),
            rows(place),
            once((1, d)),
            pl.BlockSpec((d, width), lambda i: (0, 3), pipeline_mode=pl.Buffered(1)),
        ]
        + [ANYWHERE] * len(after),
        out_specs=(rows(0), rows(0), rows(0, width), once((1, d))),
        out_shape=(
            jax.ShapeDtypeStruct((tokens, d), F32),
            jax.ShapeDtypeStruct((tokens, d), BF16),
            jax.ShapeDtypeStruct((tokens, width), BF16),
            jax.ShapeDtypeStruct((1, d), F32),
        ),
        cost_estimate=cost(
            flops=2 * tokens * d * width, bytes_accessed=2 * d * width + 16 * tokens * d, transcendentals=0
        ),
        compiler_params=pltpu.CompilerParams(vmem_limit_bytes=60 << 20),
    )(own, got, middle, dm, gain, weights, *after)


def norm_back(grad_normed, unit_rows, inverse_rows, gain):
    scaled = grad_normed * gain
    return inverse_rows * (scaled - unit_rows * jnp.mean(scaled * unit_rows, axis=1, keepdims=True))


def gather(shards):
    return lax.all_gather(jnp.concatenate(shards, 1), "seq", axis=0, tiled=True)


def per_device(
    x_in, lengths, g_attn, w_query, w_key, w_value, w_out, g_ffn, w_gate, w_up, w_down, cotangent
):
    tokens = x_in.shape[0]
    width = w_query.shape[1]
    ff = w_gate.shape[1]
    count = lax.axis_size("seq")
    def rounded(shard, a=0, b=None):
        shard = shard.astype(BF16)
        b = shard.shape[1] if b is None else b
        pad = max(0, b - shard.shape[1])
        return jnp.pad(shard[:, a:b], ((0, 0), (0, pad)))

    def zeros(n):
        return jnp.zeros((w_query.shape[0], n), BF16)

    w_down_t = w_down.astype(BF16).T
    gains_here = rounded(jnp.stack([g_attn, g_ffn], 1), 0, 128)
    attn_w = gather(
        (rounded(w_query), rounded(w_key), rounded(w_value), w_out.astype(BF16).T, gains_here)
    )
    ffn_w = []
    a = 0
    for block, steps in PARTS:
        wide = [rounded(w, a + j * block, a + (j + 1) * block) for j in range(steps) for w in (w_gate, w_up)]
        wide.append(rounded(w_down_t, a, a + steps * block))
        spare = 4224 - 3 * steps * block
        ffn_w.append(gather(wide + ([zeros(spare)] if spare > 0 else [])))
        a += steps * block
    gains = attn_w[:, 4 * width : 4 * width + 2].T.astype(F32)
    gain_one, gain_two = gains[0], gains[1]

    order = relative_blocks(count)
    first_place = lax.axis_index("seq") * tokens
    row = jnp.arange(tokens + WINDOW, dtype=jnp.int32)[:, None]
    column = jnp.arange(2 * WINDOW, dtype=jnp.int32)[None, :]
    key_place = row // WINDOW * WINDOW + column - WINDOW
    ends = [lengths[0]]
    for i in range(1, lengths.shape[0] - 1):
        ends.append(ends[-1] + lengths[i])
    seg_row = sum(((first_place + row) >= e).astype(jnp.int32) for e in ends)
    seg_key = sum(((first_place + key_place) >= e).astype(jnp.int32) for e in ends)
    allowed = (
        (key_place <= row)
        & (key_place > row - WINDOW)
        & (first_place + key_place >= 0)
        & (seg_row == seg_key)
    )
    bias = jnp.where(allowed, 0.0, -1e30).astype(F32)

    x_full = x_in.astype(F32)
    inverse_one = lax.rsqrt(jnp.mean(x_full * x_full, axis=1, keepdims=True) + EPSILON)
    unit_one = x_full * inverse_one
    def both_halves(pieces, *after):
        own, other = relative_turned(pieces, order, *after)
        return own, to_core(other)

    def both_cores(*pieces):
        return pieces, tuple(to_core(p) for p in pieces)

    def to_mp(own):
        return lax.ppermute(own, "mp", [(0, 1), (1, 0)])

    cot_turned = both_halves((cotangent,))
    normed = (unit_one * gain_one).astype(BF16)
    normed_turned = both_halves((normed,))

    qkv = rows_times((normed,), attn_w, 3 * width)
    tail = lax.ppermute(qkv[tokens - WINDOW :, width:], "seq", shift_pairs(count, 1))
    following = lax.ppermute(qkv[:WINDOW], "seq", shift_pairs(count, -1))
    mixed = attention_forward(qkv, tail, bias[:tokens])
    mixed_both = both_cores(mixed)
    branch = rows_times((mixed,), attn_w, width, 3 * width, True)
    middle = x_full + (branch.astype(F32) + to_mp(branch).astype(F32))
    inverse_two = lax.rsqrt(jnp.mean(middle * middle, axis=1, keepdims=True) + EPSILON)
    normed_two = (middle * inverse_two * gain_two).astype(BF16)
    normed_two_turned = both_halves((normed_two,))

    after = (mixed_both[1][0], cot_turned[1], normed_turned[1], following)
    one, two = (block * steps for block, steps in PARTS)
    wide_acts, hidden, *carry = feed_forward(normed_two, cotangent, ffn_w[0], PARTS[0], after=after)
    wide_acts = both_cores(wide_acts)
    one_a = weight_grad(normed_two_turned, wide_acts, (), 0, one)
    one_c = weight_grad(cot_turned, both_cores(hidden), one_a, outers=count // 4)
    one_b = weight_grad(normed_two_turned, wide_acts, one_c, one, one)
    one_c = sum_outer(one_c[0])
    places = ((0, (tokens // 128 + 1) // 2), ((tokens // 128 + 1) // 2, tokens // 256))
    after = one_b
    halves = []
    for place, blocks in places:
        halves.append(feed_forward(normed_two, cotangent, ffn_w[1], PARTS[1], tuple(carry), place, blocks, after))
        if not place:
            one_a = add_middle(one_a, (halves[0][0],))
            after = (one_a,)
    wide_acts, hidden, m_halves, dh_halves = zip(*halves)
    after = (wide_acts[1],)
    wide_acts, hidden = both_cores(*wide_acts), both_cores(*hidden)
    half = one_c.shape[0] // 2
    one_c = one_c[:half].astype(F32) + to_middle(one_c[half:]).astype(F32)
    middles = []
    for (place, _), dh in zip(places, dh_halves):
        middles.append(
            middle_gradient(dh, to_mp(dh), middle, cotangent, gain_two[None], attn_w, width, place, after)
        )
        if not place:
            two_a = weight_grad(normed_two_turned, wide_acts, (middles[0][1],), 0, two)
            da_next = lax.ppermute(middles[0][2][:WINDOW], "seq", shift_pairs(count, -1))
            after = (*two_a, da_next, one_c)
    grad_gain_two = sum(m[3][0] for m in middles)
    one_b = add_middle(one_b, (middles[1][1],))
    two_b = weight_grad(normed_two_turned, wide_acts, (one_b,), two, two)
    one_a, one_b = sum_outer(one_a), sum_outer(one_b)
    branch_turned = both_halves([m[1] for m in middles], *two_b)
    da = [m[2] for m in middles] + [da_next]
    grad_q, grad_kv = attention_backward(qkv, tail, bias, following, da, branch_turned[0])
    two_a = add_middle(two_a, (grad_q, one_a))
    two_c = weight_grad(cot_turned, hidden, (two_a,))
    two_b = add_middle(two_b, two_c)
    after = (two_b,)
    two_a, two_b = sum_outer(two_a), sum_outer(two_b)
    late, _ = lax.optimization_barrier((m_halves, branch_turned[0]))
    late = jnp.concatenate(late, 0)
    late_got = to_mp(late)
    q_part = weight_grad(normed_turned, both_cores(grad_q), after)
    kv_part = weight_grad(normed_turned, both_cores(grad_kv), (*q_part, one_b))
    own = rows_times((grad_q, grad_kv), attn_w, 3 * width, 0, True, after=kv_part)
    own_got = to_mp(own)
    out_part = weight_grad(branch_turned, mixed_both, (own, two_a))
    two_c = add_middle(two_c, (*out_part, late_got))
    q_part = add_middle(q_part, (two_c,))
    mixed_sum = sum_outer(jnp.concatenate([two_c, q_part], 1))
    down_two, q_sum = mixed_sum[:, :two], mixed_sum[:, two:].astype(F32)
    kv_part = add_middle(kv_part, (q_part, two_b))
    late_done, two_a, two_b, one_a, one_b, _ = lax.optimization_barrier(
        (late_got, two_a, two_b, one_a, one_b, kv_part)
    )
    kv_sum = sum_outer(kv_part).astype(F32)
    out_part = add_middle(out_part, (kv_part, mixed_sum))
    out_sum = sum_outer_direct(out_part)
    grad_normed = own.astype(F32) + own_got.astype(F32)
    grad_gain_one = jnp.sum(own.astype(F32) * unit_one, axis=0)
    grad_gain_one = grad_gain_one + to_mp(grad_gain_one)
    grad_middle = jnp.concatenate([m[0] for m in middles], 0)
    grad_input = grad_middle + norm_back(grad_normed, unit_one, inverse_one, gain_one)
    result = middle + (late.astype(F32) + late_done.astype(F32))
    gain_parts = jnp.stack([grad_gain_one, grad_gain_two], 0)
    gain_blocks = jnp.swapaxes(gain_parts.reshape(2, count, -1), 0, 1)
    chosen = order[:, None] == jnp.arange(count, dtype=jnp.int32)[None, :]
    gain_rel = jnp.sum(jnp.where(chosen[:, :, None, None], gain_blocks[None], 0.0), axis=1)
    gain_sums = sum_small(gain_rel)

    wide_one, wide_two = jnp.concatenate([one_a, one_b], 1), jnp.concatenate([two_a, two_b], 1)

    def columns(which):
        pieces = []
        for (block, steps), wide in zip(PARTS, (wide_one, wide_two)):
            pieces += [wide[:, (2 * j + which) * block : (2 * j + which + 1) * block] for j in range(steps)]
        return jnp.concatenate(pieces, 1)[:, :ff].astype(F32)

    grad_gate, grad_up = columns(0), columns(1)
    grad_down = jnp.concatenate([one_c, down_two.astype(F32)], 1)[:, :ff].astype(F32)

    return (
        result.astype(BF16),
        grad_input.astype(BF16),
        gain_sums[0],
        q_sum,
        kv_sum[:, :width],
        kv_sum[:, width:],
        out_sum.T,
        gain_sums[1],
        grad_gate,
        grad_up,
        grad_down.T,
    )


def solution(mesh):
    placed = (
        P("seq", None),
        P(),
        P("seq"),
        P("seq", "mp"),
        P("seq", "mp"),
        P("seq", "mp"),
        P("mp", "seq"),
        P("seq"),
        P("seq", "mp"),
        P("seq", "mp"),
        P("mp", "seq"),
        P("seq", None),
    )
    return jax.shard_map(
        per_device,
        mesh=mesh,
        in_specs=placed,
        out_specs=(
            P("seq", None),
            P("seq", None),
            P("seq"),
            P("seq", "mp"),
            P("seq", "mp"),
            P("seq", "mp"),
            P("mp", "seq"),
            P("seq"),
            P("seq", "mp"),
            P("seq", "mp"),
            P("mp", "seq"),
        ),
        check_vma=False,
    )
```

```python
import functools
import math

import jax
import jax.numpy as jnp
from jax import lax
from jax.experimental import pallas as pl
from jax.experimental.pallas import tpu as pltpu
from jax.sharding import PartitionSpec as P

HEAD_DIM = 128
WINDOW = 64
EPSILON = 1e-06
BF16 = jnp.bfloat16
F32 = jnp.float32
ANYWHERE = pl.BlockSpec(memory_space=pl.ANY)
HINT = 0.01


def cost(flops, bytes_accessed, transcendentals):
    return pl.CostEstimate(
        flops=int(HINT * flops),
        bytes_accessed=int(HINT * bytes_accessed),
        transcendentals=int(HINT * transcendentals),
    )


def mat_nn(left, right):
    return jnp.dot(left, right, preferred_element_type=F32)


def mat_nt(left, right):
    return lax.dot_general(left, right, (((1,), (1,)), ((), ())), preferred_element_type=F32)


def mat_tn(left, right):
    return lax.dot_general(left, right, (((0,), (0,)), ((), ())), preferred_element_type=F32)


def shift_pairs(count, steps):
    return [(s, s + steps) for s in range(max(0, -steps), min(count, count - steps))]


def flip_pairs(count, bit):
    return [(s, s ^ bit) for s in range(count)]


def relative_blocks(count):
    me = lax.axis_index("seq")
    place = jnp.arange(count, dtype=jnp.int32)
    outers = count // 4
    inner, middle, outer = place // (2 * outers), (place // outers) % 2, place % outers
    return (outer * 4 + ((me // 2 + middle) % 2) * 2 + (me + inner) % 2).astype(jnp.int32)


def rolled(values, steps, axis):
    return lax.dynamic_slice_in_dim(
        jnp.concatenate([values, values], axis), steps, values.shape[axis], axis
    )


def turn_blocks(pieces, order_ref, *refs):
    blocks = order_ref.shape[0] // 2
    first = 0
    for in_ref in refs[:pieces]:
        last = first + in_ref.shape[0]
        for half, out_ref in enumerate(refs[-2:]):
            for i in range(blocks):
                start = pl.multiple_of(order_ref[half * blocks + i] * 128, 128)
                out_ref[i * 128 : (i + 1) * 128, first:last] = in_ref[:, pl.ds(start, 128)].T
        first = last


def relative_turned(pieces, order, *after):
    rows, columns = sum(p.shape[0] for p in pieces), pieces[0].shape[1]
    count = order.shape[0]
    width = columns // count
    kind = pieces[0].dtype
    if width % 128:
        values = jnp.concatenate(pieces, 0)
        me, outers = lax.axis_index("seq"), count // 4
        turned = rolled(values.reshape(rows, outers, 2, 2, width), (me // 2) % 2, 2)
        turned = rolled(turned, me % 2, 3)
        return tuple(jnp.transpose(turned, (3, 2, 1, 4, 0)).reshape(2, columns // 2, rows))
    whole = pl.BlockSpec(memory_space=pltpu.VMEM)
    return pl.pallas_call(
        functools.partial(turn_blocks, len(pieces)),
        in_specs=[pl.BlockSpec(memory_space=pltpu.SMEM)] + [whole] * len(pieces) + [ANYWHERE] * len(after),
        out_specs=(whole, whole),
        out_shape=(jax.ShapeDtypeStruct((columns // 2, rows), kind),) * 2,
        cost_estimate=cost(flops=0, bytes_accessed=4 * rows * columns, transcendentals=0),
        compiler_params=pltpu.CompilerParams(vmem_limit_bytes=60 << 20),
    )(order, *pieces, *after)


def to_core(values):
    return lax.ppermute(values, "seq", flip_pairs(lax.axis_size("seq"), 1))


def to_middle(values):
    return lax.ppermute(values, "seq", flip_pairs(lax.axis_size("seq"), 2))


def sum_outer(values):
    outers = lax.axis_size("seq") // 4
    groups = [[o * 4 + place for o in range(outers)] for place in range(4)]
    return lax.psum_scatter(values, "seq", scatter_dimension=0, axis_index_groups=groups, tiled=True)


def sum_outer_direct(values):
    count = lax.axis_size("seq")
    outers = count // 4
    values = values.reshape(outers, values.shape[0] // outers, values.shape[1])
    outer = lax.axis_index("seq") // 4
    total = lax.dynamic_index_in_dim(values, outer, 0, keepdims=False).astype(F32)
    for step in range(1, outers):
        sent = lax.dynamic_index_in_dim(values, (outer + step) % outers, 0, keepdims=False)
        got = lax.ppermute(sent, "seq", [(s, (s + 4 * step) % count) for s in range(count)])
        total = total + got.astype(F32)
    return total


def add_block(keep_ref, got_ref, *refs):
    refs[-1][...] = (keep_ref[...].astype(F32) + got_ref[...].astype(F32)).astype(BF16)


def column_block(columns, most=1024):
    return next(w for w in range(most, 0, -128) if columns % w == 0)


def add_middle(part, after=()):
    keep, got = part[0], to_middle(part[1])
    rows, columns = keep.shape
    wide = column_block(columns)
    spec = pl.BlockSpec((rows, wide), lambda j: (0, j))
    return pl.pallas_call(
        add_block,
        grid=(columns // wide,),
        in_specs=[spec] * 2 + [ANYWHERE] * len(after),
        out_specs=spec,
        out_shape=jax.ShapeDtypeStruct((rows, columns), BF16),
        cost_estimate=cost(flops=rows * columns, bytes_accessed=6 * rows * columns, transcendentals=0),
        compiler_params=pltpu.CompilerParams(vmem_limit_bytes=60 << 20),
    )(keep, got, *after)


def sum_small(partial):
    count = lax.axis_size("seq")
    outers = count // 4
    rest = partial.shape[1:]
    partial = partial.reshape((2, 2 * outers) + rest)
    pair = partial[0] + to_core(partial[1])
    pair = pair.reshape((2, outers) + rest)
    four = pair[0] + to_middle(pair[1])
    outer = lax.axis_index("seq") // 4
    total = lax.dynamic_index_in_dim(four, outer, 0, keepdims=False)
    for step in range(1, outers):
        sent = lax.dynamic_index_in_dim(four, (outer + step) % outers, 0, keepdims=False)
        total = total + lax.ppermute(sent, "seq", [(s, (s + 4 * step) % count) for s in range(count)])
    return total


def bands(steps):
    return [
        (slice(i * WINDOW, (i + 1) * WINDOW), slice(i * WINDOW, (i + 2) * WINDOW)) for i in range(steps)
    ]


def band_probs(query, key, bias, steps):
    scale = 1.0 / math.sqrt(HEAD_DIM)
    scores = jnp.concatenate([mat_nt(query[rows], key[keys]) for rows, keys in bands(steps)], 0)
    scores = scores * scale + bias
    weights = jnp.exp(scores - jnp.max(scores, axis=1, keepdims=True))
    return weights / jnp.sum(weights, axis=1, keepdims=True)


def attend(q_ref, k_ref, v_ref, k_tail_ref, v_tail_ref, bias_ref, out_ref):
    steps = q_ref.shape[0] // WINDOW
    key = jnp.concatenate([k_tail_ref[...], k_ref[...]], 0)
    value = jnp.concatenate([v_tail_ref[...], v_ref[...]], 0)
    probs = band_probs(q_ref[...], key, bias_ref[...], steps).astype(BF16)
    for rows, keys in bands(steps):
        out_ref[rows] = mat_nn(probs[rows], value[keys]).astype(BF16)


def attend_back(heads, pieces, q_ref, k_ref, v_ref, k_tail_ref, v_tail_ref, bias_ref, *refs):
    q_next_ref, k_next_ref, v_next_ref = refs[:3]
    dq_ref, dkv_ref = refs[-2:]
    da = jnp.concatenate([r[...] for r in refs[3 : 4 + pieces]], 0)
    scale = 1.0 / math.sqrt(HEAD_DIM)
    head = pl.program_id(0)
    steps = da.shape[0] // WINDOW
    query = jnp.concatenate([q_ref[...], q_next_ref[...]], 0)
    key = jnp.concatenate([k_tail_ref[...], k_ref[...], k_next_ref[...]], 0)
    value = jnp.concatenate([v_tail_ref[...], v_ref[...], v_next_ref[...]], 0)
    probs = band_probs(query, key, bias_ref[...], steps)
    dp = jnp.concatenate([mat_nt(da[rows], value[keys]) for rows, keys in bands(steps)], 0)
    inner = jnp.sum(probs * dp, axis=1, keepdims=True)
    ds = (probs * (dp - inner)).astype(BF16)
    probs = probs.astype(BF16)
    low = None
    for i, (rows, keys) in enumerate(bands(steps)):
        if i < steps - 1:
            dq_ref[rows] = (mat_nn(ds[rows], key[keys]) * scale).astype(BF16)
        both = (mat_tn(ds[rows], query[rows]) * scale, mat_tn(probs[rows], da[rows]))
        if i:
            for part in range(2):
                columns = pl.ds(pl.multiple_of((part * heads + head) * HEAD_DIM, HEAD_DIM), HEAD_DIM)
                own_rows = slice((i - 1) * WINDOW, i * WINDOW)
                dkv_ref[own_rows, columns] = (both[part][:WINDOW] + low[part]).astype(BF16)
        low = [b[WINDOW:] for b in both]


def head_spec(rows, first=0):
    return pl.BlockSpec((rows, HEAD_DIM), lambda h: (0, first + h))


def once(shape):
    return pl.BlockSpec(shape, lambda j: (0, 0), pipeline_mode=pl.Buffered(1))


def attention_specs(tokens, heads, extra=0):
    return [
        head_spec(tokens),
        head_spec(tokens, heads),
        head_spec(tokens, 2 * heads),
        head_spec(WINDOW),
        head_spec(WINDOW, heads),
        once((tokens + extra, 2 * WINDOW)),
    ]


def attention_forward(qkv, tail, bias):
    tokens, heads = qkv.shape[0], qkv.shape[1] // (3 * HEAD_DIM)
    width = heads * HEAD_DIM
    return pl.pallas_call(
        attend,
        grid=(heads,),
        in_specs=attention_specs(tokens, heads),
        out_specs=head_spec(tokens),
        out_shape=jax.ShapeDtypeStruct((tokens, width), BF16),
        cost_estimate=cost(
            flops=8 * tokens * width * WINDOW, bytes_accessed=8 * tokens * width, transcendentals=tokens * width
        ),
        compiler_params=pltpu.CompilerParams(vmem_limit_bytes=60 << 20),
    )(qkv, qkv, qkv, tail, tail, bias)


def attention_backward(qkv, tail, bias, following, da, *after):
    tokens, heads = qkv.shape[0], qkv.shape[1] // (3 * HEAD_DIM)
    width = heads * HEAD_DIM
    return pl.pallas_call(
        functools.partial(attend_back, heads, len(da) - 1),
        grid=(heads,),
        in_specs=attention_specs(tokens, heads, WINDOW)
        + [head_spec(WINDOW, part * heads) for part in range(3)]
        + [head_spec(d.shape[0]) for d in da]
        + [ANYWHERE] * len(after),
        out_specs=(head_spec(tokens), once((tokens, 2 * width))),
        out_shape=(
            jax.ShapeDtypeStruct((tokens, width), BF16),
            jax.ShapeDtypeStruct((tokens, 2 * width), BF16),
        ),
        cost_estimate=cost(
            flops=20 * tokens * width * WINDOW, bytes_accessed=14 * tokens * width, transcendentals=tokens * width
        ),
        compiler_params=pltpu.CompilerParams(vmem_limit_bytes=60 << 20),
    )(qkv, qkv, qkv, tail, tail, bias, following, following, following, *da, *after)


def multiply(turned, pieces, *refs):
    w_ref = refs[pieces]
    total, first = None, 0
    for x_ref in refs[:pieces]:
        last = first + x_ref.shape[1]
        term = mat_nt(x_ref[...], w_ref[:, first:last]) if turned else mat_nn(x_ref[...], w_ref[...])
        total = term if total is None else total + term
        first = last
    refs[-1][...] = total.astype(BF16)


def rows_times(pieces, weights, columns, first=0, turned=False, wide=512, after=()):
    tokens, d = pieces[0].shape[0], sum(p.shape[1] for p in pieces)
    if turned:
        out = weights.shape[0]
        spec = pl.BlockSpec((wide, columns), lambda j: (j, first // columns))
    else:
        out = columns
        spec = pl.BlockSpec((d, wide), lambda j: (0, first // wide + j))
    return pl.pallas_call(
        functools.partial(multiply, turned, len(pieces)),
        grid=(out // wide,),
        in_specs=[once(p.shape) for p in pieces] + [spec] + [ANYWHERE] * len(after),
        out_specs=pl.BlockSpec((tokens, wide), lambda j: (0, j)),
        out_shape=jax.ShapeDtypeStruct((tokens, out), BF16),
        cost_estimate=cost(
            flops=2 * tokens * d * out, bytes_accessed=2 * (tokens * (d + out) + d * out), transcendentals=0
        ),
        compiler_params=pltpu.CompilerParams(vmem_limit_bytes=60 << 20),
    )(*pieces, weights, *after)


PARTS = ((768, 2), (1280, 1))


def feed(block, steps, first_row, h_ref, dm_ref, wgu_ref, wd_ref, *refs):
    j = pl.program_id(0)
    carried = first_row is not None
    if carried:
        m_in, dh_in = refs[:2]
        wide_ref, hidden_ref, m_out, dh_out, m_sum, dh_sum, m_sem, dh_sem = refs[-8:]
        here = pl.ds(first_row, m_sum.shape[0])
        copies = (
            pltpu.make_async_copy(m_in.at[here], m_sum, m_sem),
            pltpu.make_async_copy(dh_in.at[here], dh_sum, dh_sem),
        )

        @pl.when(j == 0)
        def _():
            for copy in copies:
                copy.start()

    else:
        wide_ref, hidden_ref, m_sum, dh_sum = refs[-4:]
    taken = slice(first_row or 0, (first_row or 0) + m_sum.shape[0])
    gate_up = mat_nn(h_ref[taken], wgu_ref[...])
    gate, up = gate_up[:, :block], gate_up[:, block:]
    dhidden = mat_nn(dm_ref[taken], wd_ref[...])
    sigma = jax.nn.sigmoid(gate)
    silu = gate * sigma
    hidden = (silu * up).astype(BF16)
    dup = (dhidden * silu).astype(BF16)
    dgate = (dhidden * up * (sigma * (1.0 + gate * (1.0 - sigma)))).astype(BF16)
    dgate_up = jnp.concatenate([dgate, dup], 1)
    wide_ref[...] = dgate_up
    hidden_ref[...] = hidden

    @pl.when(j == 0)
    def _():
        if carried:
            for copy in copies:
                copy.wait()
        else:
            m_sum[...] = jnp.zeros_like(m_sum)
            dh_sum[...] = jnp.zeros_like(dh_sum)

    width = 512
    for c in range(0, m_sum.shape[1], width):
        part = slice(c, c + width)
        dh_sum[:, part] += mat_nt(dgate_up, wgu_ref[part])
        m_sum[:, part] += mat_nt(hidden, wd_ref[part])

    if carried:

        @pl.when(j == steps - 1)
        def _():
            m_out[...] = m_sum[...].astype(BF16)
            dh_out[...] = dh_sum[...].astype(BF16)


def feed_forward(rows, dm, weights, part, carry=(), place=0, count=1, after=()):
    d = rows.shape[1]
    block, steps = part
    wide = steps * block
    carried = bool(carry)
    tokens = count * 128 if carried else rows.shape[0]
    row_spec = once((tokens, d))
    kind = BF16 if carried else F32
    return pl.pallas_call(
        functools.partial(feed, block, steps, place * 128 if carried else None),
        grid=(steps,),
        in_specs=[
            once(rows.shape),
            once(rows.shape),
            pl.BlockSpec((d, 2 * block), lambda j: (0, j)),
            pl.BlockSpec((d, block), lambda j: (0, 2 * steps + j)),
        ]
        + [ANYWHERE] * (len(carry) + len(after)),
        out_specs=(
            pl.BlockSpec((tokens, 2 * block), lambda j: (0, j)),
            pl.BlockSpec((tokens, block), lambda j: (0, j)),
            row_spec,
            row_spec,
        ),
        out_shape=(
            jax.ShapeDtypeStruct((tokens, 2 * wide), BF16),
            jax.ShapeDtypeStruct((tokens, wide), BF16),
            jax.ShapeDtypeStruct((tokens, d), kind),
            jax.ShapeDtypeStruct((tokens, d), kind),
        ),
        scratch_shapes=([pltpu.VMEM((tokens, d), F32)] * 2 + [pltpu.SemaphoreType.DMA] * 2) if carried else [],
        cost_estimate=cost(
            flops=12 * tokens * d * wide, bytes_accessed=6 * d * wide + 24 * tokens * d, transcendentals=tokens * wide
        ),
        compiler_params=pltpu.CompilerParams(vmem_limit_bytes=60 << 20),
    )(rows, dm, weights, weights, *carry, *after)


def grad_block(pieces, outers, left_ref, left_got_ref, *refs):
    keep_ref, send_ref = refs[-2:]
    total = None
    for side, left in enumerate((left_ref, left_got_ref)):
        first = 0
        for right in refs[side * pieces : (side + 1) * pieces]:
            last = first + right.shape[0]
            term = mat_nn(left[:, first:last], right[...])
            total = term if total is None else total + term
            first = last
    total = total.astype(BF16)
    half = total.shape[0] // 2
    if not outers:
        keep_ref[...] = total[:half]
        send_ref[...] = total[half:]
        return
    block = half // outers
    for i in range(2 * outers):
        first = (i % 2) * half + (i // 2) * block
        send_ref[i * block : (i + 1) * block] = total[first : first + block]


def weight_grad(left, right, after=(), first=0, columns=None, outers=0):
    d, tokens = left[0].shape
    columns = columns or right[0][0].shape[1]
    wide = next(w for w in (640, 512, 256, 128) if columns % w == 0 and first % w == 0)
    pieces = tuple(right[0]) + tuple(right[1])
    outs = (jax.ShapeDtypeStruct((d, columns), BF16),)
    if not outers:
        outs = (jax.ShapeDtypeStruct((d // 2, columns), BF16),) * 2
    return pl.pallas_call(
        functools.partial(grad_block, len(right[0]), outers),
        grid=(columns // wide,),
        in_specs=[once((d, tokens))] * 2
        + [pl.BlockSpec((p.shape[0], wide), lambda j: (0, first // wide + j)) for p in pieces]
        + [ANYWHERE] * len(after),
        out_specs=(pl.BlockSpec((d // len(outs), wide), lambda j: (0, j)),) * len(outs),
        out_shape=outs,
        cost_estimate=cost(
            flops=4 * tokens * d * columns, bytes_accessed=2 * (d + 2 * tokens) * columns + 4 * d * tokens, transcendentals=0
        ),
        compiler_params=pltpu.CompilerParams(vmem_limit_bytes=60 << 20),
    )(*left, *pieces, *after)


def middle_back(own_ref, got_ref, middle_ref, dm_ref, gain_ref, wo_ref, *refs):
    grad_ref, low_ref, da_ref, gain_out = refs[-4:]
    rows = middle_ref[...]
    inverse = lax.rsqrt(jnp.mean(rows * rows, axis=1, keepdims=True) + EPSILON)
    unit = rows * inverse
    dh = own_ref[...].astype(F32) + got_ref[...].astype(F32)
    grad = dm_ref[...].astype(F32) + norm_back(dh, unit, inverse, gain_ref[...])
    grad_ref[...] = grad
    low = grad.astype(BF16)
    low_ref[...] = low
    da_ref[...] = mat_nn(low, wo_ref[...]).astype(BF16)
    part = jnp.sum(dh * unit, axis=0, keepdims=True)

    @pl.when(pl.program_id(0) == 0)
    def _():
        gain_out[...] = part

    @pl.when(pl.program_id(0) > 0)
    def _():
        gain_out[...] += part


def middle_gradient(own, got, middle, dm, gain, weights, width, place, after=()):
    tokens, d = own.shape

    def rows(first, n=d):
        return pl.BlockSpec((128, n), lambda i: (first + i, 0))

    return pl.pallas_call(
        middle_back,
        grid=(tokens // 128,),
        in_specs=[
            rows(0),
            rows(0),
            rows(place),
            rows(place),
            once((1, d)),
            pl.BlockSpec((d, width), lambda i: (0, 3), pipeline_mode=pl.Buffered(1)),
        ]
        + [ANYWHERE] * len(after),
        out_specs=(rows(0), rows(0), rows(0, width), once((1, d))),
        out_shape=(
            jax.ShapeDtypeStruct((tokens, d), F32),
            jax.ShapeDtypeStruct((tokens, d), BF16),
            jax.ShapeDtypeStruct((tokens, width), BF16),
            jax.ShapeDtypeStruct((1, d), F32),
        ),
        cost_estimate=cost(
            flops=2 * tokens * d * width, bytes_accessed=2 * d * width + 16 * tokens * d, transcendentals=0
        ),
        compiler_params=pltpu.CompilerParams(vmem_limit_bytes=60 << 20),
    )(own, got, middle, dm, gain, weights, *after)


def norm_back(grad_normed, unit_rows, inverse_rows, gain):
    scaled = grad_normed * gain
    return inverse_rows * (scaled - unit_rows * jnp.mean(scaled * unit_rows, axis=1, keepdims=True))


def gather(shards):
    return lax.all_gather(jnp.concatenate(shards, 1), "seq", axis=0, tiled=True)


def per_device(
    x_in, lengths, g_attn, w_query, w_key, w_value, w_out, g_ffn, w_gate, w_up, w_down, cotangent
):
    tokens = x_in.shape[0]
    width = w_query.shape[1]
    ff = w_gate.shape[1]
    count = lax.axis_size("seq")
    def rounded(shard, a=0, b=None):
        shard = shard.astype(BF16)
        b = shard.shape[1] if b is None else b
        pad = max(0, b - shard.shape[1])
        return jnp.pad(shard[:, a:b], ((0, 0), (0, pad)))

    def zeros(n):
        return jnp.zeros((w_query.shape[0], n), BF16)

    w_down_t = w_down.astype(BF16).T
    gains_here = rounded(jnp.stack([g_attn, g_ffn], 1), 0, 128)
    attn_w = gather(
        (rounded(w_query), rounded(w_key), rounded(w_value), w_out.astype(BF16).T, gains_here)
    )
    ffn_w = []
    a = 0
    for block, steps in PARTS:
        wide = [rounded(w, a + j * block, a + (j + 1) * block) for j in range(steps) for w in (w_gate, w_up)]
        wide.append(rounded(w_down_t, a, a + steps * block))
        spare = 4224 - 3 * steps * block
        ffn_w.append(gather(wide + ([zeros(spare)] if spare > 0 else [])))
        a += steps * block
    gains = attn_w[:, 4 * width : 4 * width + 2].T.astype(F32)
    gain_one, gain_two = gains[0], gains[1]

    order = relative_blocks(count)
    first_place = lax.axis_index("seq") * tokens
    row = jnp.arange(tokens + WINDOW, dtype=jnp.int32)[:, None]
    column = jnp.arange(2 * WINDOW, dtype=jnp.int32)[None, :]
    key_place = row // WINDOW * WINDOW + column - WINDOW
    ends = [lengths[0]]
    for i in range(1, lengths.shape[0] - 1):
        ends.append(ends[-1] + lengths[i])
    seg_row = sum(((first_place + row) >= e).astype(jnp.int32) for e in ends)
    seg_key = sum(((first_place + key_place) >= e).astype(jnp.int32) for e in ends)
    allowed = (
        (key_place <= row)
        & (key_place > row - WINDOW)
        & (first_place + key_place >= 0)
        & (seg_row == seg_key)
    )
    bias = jnp.where(allowed, 0.0, -1e30).astype(F32)

    x_full = x_in.astype(F32)
    inverse_one = lax.rsqrt(jnp.mean(x_full * x_full, axis=1, keepdims=True) + EPSILON)
    unit_one = x_full * inverse_one
    def both_halves(pieces, *after):
        own, other = relative_turned(pieces, order, *after)
        return own, to_core(other)

    def both_cores(*pieces):
        return pieces, tuple(to_core(p) for p in pieces)

    def to_mp(own):
        return lax.ppermute(own, "mp", [(0, 1), (1, 0)])

    cot_turned = both_halves((cotangent,))
    normed = (unit_one * gain_one).astype(BF16)
    normed_turned = both_halves((normed,))

    qkv = rows_times((normed,), attn_w, 3 * width)
    tail = lax.ppermute(qkv[tokens - WINDOW :, width:], "seq", shift_pairs(count, 1))
    following = lax.ppermute(qkv[:WINDOW], "seq", shift_pairs(count, -1))
    mixed = attention_forward(qkv, tail, bias[:tokens])
    mixed_both = both_cores(mixed)
    branch = rows_times((mixed,), attn_w, width, 3 * width, True)
    middle = x_full + (branch.astype(F32) + to_mp(branch).astype(F32))
    inverse_two = lax.rsqrt(jnp.mean(middle * middle, axis=1, keepdims=True) + EPSILON)
    normed_two = (middle * inverse_two * gain_two).astype(BF16)
    normed_two_turned = both_halves((normed_two,))

    after = (mixed_both[1][0], cot_turned[1], normed_turned[1], following)
    one, two = (block * steps for block, steps in PARTS)
    wide_acts, hidden, *carry = feed_forward(normed_two, cotangent, ffn_w[0], PARTS[0], after=after)
    wide_acts = both_cores(wide_acts)
    one_a = weight_grad(normed_two_turned, wide_acts, (), 0, one)
    one_c = weight_grad(cot_turned, both_cores(hidden), one_a, outers=count // 4)
    one_b = weight_grad(normed_two_turned, wide_acts, one_c, one, one)
    one_c = sum_outer(one_c[0])
    places = ((0, (tokens // 128 + 1) // 2), ((tokens // 128 + 1) // 2, tokens // 256))
    after = one_b
    halves = []
    for place, blocks in places:
        halves.append(feed_forward(normed_two, cotangent, ffn_w[1], PARTS[1], tuple(carry), place, blocks, after))
        if not place:
            one_a = add_middle(one_a, (halves[0][0],))
            after = (one_a,)
    wide_acts, hidden, m_halves, dh_halves = zip(*halves)
    after = (wide_acts[1],)
    wide_acts, hidden = both_cores(*wide_acts), both_cores(*hidden)
    half = one_c.shape[0] // 2
    one_c = one_c[:half].astype(F32) + to_middle(one_c[half:]).astype(F32)
    middles = []
    for (place, _), dh in zip(places, dh_halves):
        middles.append(
            middle_gradient(dh, to_mp(dh), middle, cotangent, gain_two[None], attn_w, width, place, after)
        )
        if not place:
            two_a = weight_grad(normed_two_turned, wide_acts, (middles[0][1],), 0, two)
            da_next = lax.ppermute(middles[0][2][:WINDOW], "seq", shift_pairs(count, -1))
            after = (*two_a, da_next, one_c)
    grad_gain_two = sum(m[3][0] for m in middles)
    one_b = add_middle(one_b, (middles[1][1],))
    two_b = weight_grad(normed_two_turned, wide_acts, (one_b,), two, two)
    one_a, one_b = sum_outer(one_a), sum_outer(one_b)
    branch_turned = both_halves([m[1] for m in middles], *two_b)
    da = [m[2] for m in middles] + [da_next]
    grad_q, grad_kv = attention_backward(qkv, tail, bias, following, da, branch_turned[0])
    two_a = add_middle(two_a, (grad_q, one_a))
    two_c = weight_grad(cot_turned, hidden, (two_a,))
    two_b = add_middle(two_b, two_c)
    after = (two_b,)
    two_a, two_b = sum_outer(two_a), sum_outer(two_b)
    late, _ = lax.optimization_barrier((m_halves, branch_turned[0]))
    late = jnp.concatenate(late, 0)
    late_got = to_mp(late)
    q_part = weight_grad(normed_turned, both_cores(grad_q), after)
    kv_part = weight_grad(normed_turned, both_cores(grad_kv), (*q_part, one_b))
    own = rows_times((grad_q, grad_kv), attn_w, 3 * width, 0, True, after=kv_part)
    own_got = to_mp(own)
    out_part = weight_grad(branch_turned, mixed_both, (own, two_a))
    two_c = add_middle(two_c, (*out_part, late_got))
    q_part = add_middle(q_part, (two_c,))
    mixed_sum = sum_outer(jnp.concatenate([two_c, q_part], 1))
    down_two, q_sum = mixed_sum[:, :two], mixed_sum[:, two:].astype(F32)
    kv_part = add_middle(kv_part, (q_part, two_b))
    late_done, two_a, two_b, one_a, one_b, _ = lax.optimization_barrier(
        (late_got, two_a, two_b, one_a, one_b, kv_part)
    )
    kv_sum = sum_outer(kv_part).astype(F32)
    out_part = add_middle(out_part, (kv_part, mixed_sum))
    out_sum = sum_outer_direct(out_part)
    grad_normed = own.astype(F32) + own_got.astype(F32)
    grad_gain_one = jnp.sum(own.astype(F32) * unit_one, axis=0)
    grad_gain_one = grad_gain_one + to_mp(grad_gain_one)
    grad_middle = jnp.concatenate([m[0] for m in middles], 0)
    grad_input = grad_middle + norm_back(grad_normed, unit_one, inverse_one, gain_one)
    result = middle + (late.astype(F32) + late_done.astype(F32))
    gain_parts = jnp.stack([grad_gain_one, grad_gain_two], 0)
    gain_blocks = jnp.swapaxes(gain_parts.reshape(2, count, -1), 0, 1)
    chosen = order[:, None] == jnp.arange(count, dtype=jnp.int32)[None, :]
    gain_rel = jnp.sum(jnp.where(chosen[:, :, None, None], gain_blocks[None], 0.0), axis=1)
    gain_sums = sum_small(gain_rel)

    wide_one, wide_two = jnp.concatenate([one_a, one_b], 1), jnp.concatenate([two_a, two_b], 1)

    def columns(which):
        pieces = []
        for (block, steps), wide in zip(PARTS, (wide_one, wide_two)):
            pieces += [wide[:, (2 * j + which) * block : (2 * j + which + 1) * block] for j in range(steps)]
        return jnp.concatenate(pieces, 1)[:, :ff].astype(F32)

    grad_gate, grad_up = columns(0), columns(1)
    grad_down = jnp.concatenate([one_c, down_two.astype(F32)], 1)[:, :ff].astype(F32)

    return (
        result.astype(BF16),
        grad_input.astype(BF16),
        gain_sums[0],
        q_sum,
        kv_sum[:, :width],
        kv_sum[:, width:],
        out_sum.T,
        gain_sums[1],
        grad_gate,
        grad_up,
        grad_down.T,
    )


def solution(mesh):
    placed = (
        P("seq", None),
        P(),
        P("seq"),
        P("seq", "mp"),
        P("seq", "mp"),
        P("seq", "mp"),
        P("mp", "seq"),
        P("seq"),
        P("seq", "mp"),
        P("seq", "mp"),
        P("mp", "seq"),
        P("seq", None),
    )
    return jax.shard_map(
        per_device,
        mesh=mesh,
        in_specs=placed,
        out_specs=(
            P("seq", None),
            P("seq", None),
            P("seq"),
            P("seq", "mp"),
            P("seq", "mp"),
            P("seq", "mp"),
            P("mp", "seq"),
            P("seq"),
            P("seq", "mp"),
            P("seq", "mp"),
            P("mp", "seq"),
        ),
        check_vma=False,
    )
```
